32 devices in a mesh: users: 4 (over y, x), ctx: 8 (over z, core).
Axes of the slice: x: 2, y: 2, z: 4, core: 2. Of those that a mesh axis runs over, the one named last changes fastest.
Arguments:
- cand_feat: bfloat16 [12288, 1024], P(('users', 'ctx')), may hold values from -27 to 27
- cand_user: int32 [12288, 1], P(('users', 'ctx')), may hold values from 0 to 3; in each aligned block of 384 rows (0 to 383, 384 to 767, ...) at most 192 rows name the same one
- hist_kv: bfloat16 [1, 4, 1024, 2048], P(None, 'users', 'ctx'), may hold values from -27 to 27
- hist_mask: int32 [4, 8], P('users'), may hold values from 0 to 1, as said below
- gain_in: float32 [1, 1024], replicated, may hold values from 0.25 to 1.75
- w_uq: bfloat16 [1, 1024, 2048], replicated, may hold values from -0.1875 to 0.1875
- gain_attn: float32 [1, 1024], replicated, may hold values from 0.25 to 1.75
- w_out: bfloat16 [1, 1024, 1024], replicated, may hold values from -0.1875 to 0.1875
Outputs:
- cand_out: bfloat16 [12288, 1024], P(('users', 'ctx'))
The draws below stay inside these ranges and needn't reach their ends.
Inputs may be any that keep to these rules, and one draw needn't show every extreme that they name: `cand_user`: within the rows of one device no user is named by more than 192 rows, a bound that some block reaches of them. `hist_mask`: every user has exactly 4 ones among its 8 blocks.
All inputs are finite; a program needn't handle non-finite values.
Results may differ from the reference program's by a relative error of at most 0.0039.
Values may be sent and summed in bfloat16 or wider, within the bound.
No kernel may reach another device: no remote copies, remote signals or barrier semaphores. Data moves between devices by JAX's collectives and lax.ppermute only.
A program may use at most 128 MiB of HBM per device.

```python
import math
import jax
import jax.numpy as jnp
import numpy as np
from jax import lax

D = 1024
H = 8
BLK = 128
LAYERS = 1
SRC_ROWS = 384
USERS = 4
ROWS = 12288
HIST = 1024
NBLK = 8
LIVE = 4
MOST = 192
USER_CAP = 6144


def log_scale(key, shape):
    return jnp.exp(jax.random.uniform(key, shape, jnp.float32, math.log(0.3), math.log(3.0)))


def draw_cand_feat(key, part):
    key_main = jax.random.fold_in(key, 0)
    key_rows = jax.random.fold_in(key, 2)
    key_cols = jax.random.fold_in(key, 3)
    noise = jnp.clip(jax.random.normal(key_main, (ROWS, D), jnp.float32), -3.0, 3.0)
    scaled = noise * log_scale(key_rows, (ROWS, 1)) * log_scale(key_cols, (1, D))
    return scaled.astype(jnp.bfloat16)


def draw_hist_kv(key, part):
    key_main = jax.random.fold_in(key, 0)
    key_rows = jax.random.fold_in(key, 2)
    key_cols = jax.random.fold_in(key, 3)
    full_shape = (LAYERS, USERS, HIST, 2 * D)
    noise = jnp.clip(jax.random.normal(key_main, full_shape, jnp.float32), -3.0, 3.0)
    is_value = jnp.arange(2 * D) >= D
    column_scale = jnp.where(is_value, log_scale(key_cols, (2 * D,)), 1.0)
    row_scale = jnp.where(is_value, log_scale(key_rows, (LAYERS, USERS, HIST, 1)), 1.0)
    return (noise * column_scale * row_scale).astype(jnp.bfloat16)


def draw_hist_mask(key, part):
    user_keys = jax.random.split(key, USERS)
    orders = jax.vmap(lambda user_key: jax.random.permutation(user_key, NBLK))(user_keys)
    return (orders < LIVE).astype(jnp.int32)


def assign_block(stream_key, own, number, rows, count, top, reach, lean):
    ranking = jax.random.permutation(stream_key, count)
    crowded, ordinary = portions_of(count, rows * top, reach, lean, True), portions_of(count, rows * top, reach, lean, False)
    places = jnp.arange(count)

    def named(lengths, offset_by):
        used = int((lengths > 0).sum())
        fixed = max(1, used // 4)
        passed = fixed + (places - fixed + offset_by * (used - fixed)) % max(1, count - fixed)
        return jnp.zeros((count,), jnp.int32).at[ranking[jnp.where(places < fixed, places, passed)]].set(jnp.asarray(lengths, jnp.int32))

    lengths = jnp.where(number % 4 == 0, named(crowded, number // 4), named(ordinary, number - number // 4 - 1))
    mixed = jax.random.permutation(jax.random.fold_in(own, 3), count)
    donor, taker = mixed[0:count // 2 * 2:2], mixed[1:count // 2 * 2:2]
    slack = jnp.minimum(lengths[donor] - 1, reach - lengths[taker]) // 2
    slack = jnp.where((donor == ranking[0]) | (taker == ranking[0]) | (lengths[taker] == 0), 0, jnp.maximum(slack, 0))
    passed = jax.random.randint(jax.random.fold_in(own, 4), (count // 2,), 0, 1 << 20) % (slack + 1)
    lengths = lengths.at[donor].add(-passed).at[taker].add(passed)
    items = jnp.searchsorted(jnp.cumsum(lengths), jnp.arange(rows * top), side="right").astype(jnp.int32)
    table = items.reshape(top, rows).T
    table = table[jax.random.permutation(jax.random.fold_in(own, 1), rows)]
    offset_by = jax.random.randint(jax.random.fold_in(own, 2), (rows, 1), 0, top)
    return jnp.take_along_axis(table, (jnp.arange(top)[None, :] + offset_by) % top, axis=1)


def portions_of(amount, total, limit, slope, full):
    weights = [(1 << 20) // math.isqrt(standing ** slope) + 1 for standing in range(1, amount + 1)]
    largest = limit if full else min(limit, max(-(-total // amount), total * weights[0] // sum(weights)))
    least = 1 if total - largest >= amount - 1 else 0
    counts, rest = [largest] + [least] * (amount - 1), total - largest - least * (amount - 1)
    while rest > 0:
        candidates = [i for i in range(1, amount) if counts[i] < largest] or [i for i in range(1, amount) if counts[i] < limit]
        pool, remaining = sum([weights[i] for i in candidates]), rest
        for i in candidates:
            addition = min(limit - counts[i], max(1, remaining * weights[i] // pool), rest)
            counts[i] = counts[i] + addition
            rest = rest - addition
    return np.array(counts)


def bell_draw(key, dims, scale, bound, kind=jnp.bfloat16):
    entries = jax.random.normal(key, dims, jnp.float32) * scale
    return jnp.minimum(jnp.maximum(entries, -bound), bound).astype(kind)


def setup_inputs(seed: int = 0) -> dict:
    splits = jax.random.split(jax.random.key(seed), 9)
    cand_feat = draw_cand_feat(jax.random.fold_in(splits[8], 71), 0)
    cand_user_keys = jax.random.split(jax.random.fold_in(splits[1], 1), ROWS // SRC_ROWS)
    cand_user_turns = jax.random.permutation(jax.random.fold_in(splits[1], 3), ROWS // SRC_ROWS)
    cand_user = jax.vmap(lambda own, number: assign_block(jax.random.fold_in(splits[1], 2), own, number, SRC_ROWS, USERS, 1, MOST, 2))(cand_user_keys, cand_user_turns).reshape((ROWS, 1))
    hist_kv = draw_hist_kv(jax.random.fold_in(splits[8], 71), 0)
    hist_mask = draw_hist_mask(jax.random.fold_in(splits[8], 71), 0)
    gain_in = jnp.clip(1.0 + 0.15 * jax.random.normal(splits[4], (LAYERS, D), jnp.float32), 0.25, 1.75)
    w_uq = bell_draw(splits[5], (LAYERS, D, 2 * D), D ** -0.5, 0.1875)
    gain_attn = jnp.clip(1.0 + 0.15 * jax.random.normal(splits[6], (LAYERS, D), jnp.float32), 0.25, 1.75)
    w_out = bell_draw(splits[7], (LAYERS, D, D), D ** -0.5, 0.1875)
    return dict(cand_feat=cand_feat, cand_user=cand_user, hist_kv=hist_kv, hist_mask=hist_mask, gain_in=gain_in, w_uq=w_uq, gain_attn=gain_attn, w_out=w_out)


def centred_norm(inputs):
    middle = lax.optimization_barrier(jnp.mean(inputs, axis=-1, keepdims=True))
    shifted = inputs - middle
    spread = lax.optimization_barrier(jnp.mean(shifted * shifted, axis=-1, keepdims=True))
    return shifted * lax.rsqrt(spread + 1e-05)

def score_user(queries, kv_rows):
    capacity = queries.shape[0]
    head_size = D // H
    query_heads = queries.reshape(capacity, H, head_size).transpose(1, 0, 2)
    key_heads = kv_rows[:, :D].reshape(-1, H, head_size).transpose(1, 0, 2)
    value_heads = kv_rows[:, D:].reshape(-1, H, head_size).transpose(1, 0, 2)

    def one_head(packed):
        query_part, key_part, value_part = packed
        scores = jnp.dot(query_part, key_part.T, preferred_element_type=jnp.float32) * head_size ** (-0.5)
        attn_weights = jax.nn.silu(scores).astype(jnp.bfloat16)
        return jnp.dot(attn_weights, value_part, preferred_element_type=jnp.float32)
    combined = lax.map(one_head, (query_heads, key_heads, value_heads))
    return combined.transpose(1, 0, 2).reshape(capacity, D)

def reference(cand_feat, cand_user, hist_kv, hist_mask, gain_in, w_uq, gain_attn, w_out):
    owner_ids = cand_user[:, 0]
    user_range = jnp.arange(USERS, dtype=jnp.int32)
    sorted_rows = jnp.argsort(owner_ids, stable=True).astype(jnp.int32)
    user_counts = lax.optimization_barrier(jnp.sum((owner_ids[:, None] == user_range[None, :]).astype(jnp.int32), axis=0)).astype(jnp.int32)
    user_starts = (jnp.cumsum(user_counts) - user_counts).astype(jnp.int32)
    slot_offsets = jnp.arange(USER_CAP, dtype=jnp.int32)
    positions = jnp.minimum(user_starts[:, None] + slot_offsets[None, :], ROWS - 1).astype(jnp.int32)
    members = sorted_rows[positions]
    in_range = (slot_offsets[None, :] < user_counts[:, None]).astype(jnp.float32)
    live_blocks = jnp.argsort(1 - hist_mask, axis=1, stable=True)[:, :LIVE].astype(jnp.int32)
    hidden = cand_feat
    for layer_index in range(LAYERS):
        residual = hidden.astype(jnp.float32)
        normed = (centred_norm(residual) * gain_in[layer_index]).astype(jnp.bfloat16)
        projected = jnp.dot(normed, w_uq[layer_index], preferred_element_type=jnp.float32)
        gate_vals = jax.nn.silu(projected[:, :D])
        queries = jax.nn.silu(projected[:, D:]).astype(jnp.bfloat16)
        layer_kv = hist_kv[layer_index]

        def add_user(user_index, running):
            picked = queries[members[user_index]]
            user_kv = layer_kv[user_index].reshape(NBLK, BLK, 2 * D)[live_blocks[user_index]].reshape(LIVE * BLK, 2 * D)
            scored = score_user(picked, user_kv) * in_range[user_index][:, None]
            return running.at[members[user_index]].add(scored)
        attended = lax.fori_loop(0, USERS, add_user, jnp.zeros((ROWS, D), jnp.float32))
        mixed = (centred_norm(attended) * gain_attn[layer_index] * gate_vals).astype(jnp.bfloat16)
        hidden = (residual + jnp.dot(mixed, w_out[layer_index], preferred_element_type=jnp.float32)).astype(jnp.bfloat16)
    return hidden
```

```python
import functools

import jax
import jax.numpy as jnp
from jax import lax
from jax.experimental import pallas as pl
from jax.experimental.pallas import tpu as pltpu
from jax.sharding import PartitionSpec as P

BLK = 128
HEAD = 128
CHUNKS = 2
VMEM_LIMIT = 56 * 1024 * 1024


def silu_halved(t):
    return t + t * jnp.tanh(t)


def centred_norm(x):
    middle = jnp.mean(x, axis=-1, keepdims=True)
    shifted = x - middle
    spread = jnp.mean(shifted * shifted, axis=-1, keepdims=True)
    return shifted * lax.rsqrt(spread + 1e-05)


def slots_of(user, me, cap):
    rows = user.shape[0]
    rel = user ^ me
    lanes = lax.broadcasted_iota(jnp.int32, (rows, 128), 1)
    one_hot = (rel == lanes).astype(jnp.float32)
    above = lax.broadcasted_iota(jnp.int32, (rows, rows), 0)
    below = lax.broadcasted_iota(jnp.int32, (rows, rows), 1)
    earlier = (below < above).astype(jnp.bfloat16)
    rank = jnp.dot(earlier, one_hot.astype(jnp.bfloat16), preferred_element_type=jnp.float32)
    rank = jnp.sum(rank * one_hot, axis=1, keepdims=True)
    return rel.astype(jnp.float32) * cap + rank


def kv_split_kernel(chunks, ids, kv, *outs):
    core = ids[1]
    half = kv.shape[1] // 4
    wide = half // chunks
    for chunk in range(chunks):
        for swap in range(2):
            side = core if swap == 0 else 1 - core
            out = outs[2 * chunk + swap]
            for part in range(2):
                at = pl.multiple_of(part * 2 * half + side * half + chunk * wide, 128)
                out[:, part * wide:(part + 1) * wide] = kv[:, pl.ds(at, wide)]


def query_kernel(chunks, cap, ids, feat, user, gain, wq, normed_out, *rest):
    outs, halves = rest[:-1], rest[-1]
    me, core = ids[0], ids[1]
    rows, width = feat.shape
    half = width // 2
    wide = half // chunks
    users = rows * 2 // cap
    normed = (centred_norm(feat[...].astype(jnp.float32)) * gain[...]).astype(jnp.bfloat16)
    normed_out[...] = normed
    slot = slots_of(user[...], me, cap)
    slot_row = jnp.transpose(jnp.broadcast_to(slot, (rows, 128)))[0:1, :]
    places = lax.broadcasted_iota(jnp.int32, (users * cap, rows), 0).astype(jnp.float32)
    pick = (places == slot_row).astype(jnp.bfloat16)
    for side in range(2):
        part = jnp.dot(
            normed, wq[:, side * half:(side + 1) * half], preferred_element_type=jnp.float32
        )
        halves[side] = silu_halved(part * 0.5).astype(jnp.bfloat16)
    for swap in range(2):
        side = core if swap == 0 else 1 - core
        sent = jnp.dot(pick, halves[side], preferred_element_type=jnp.float32).astype(jnp.bfloat16)
        for chunk in range(chunks):
            for d in range(users):
                outs[(chunk * 2 + swap) * users + d][...] = sent[
                    d * cap:(d + 1) * cap, chunk * wide:(chunk + 1) * wide
                ]


def gate_kernel(normed, wg, out):
    part = jnp.dot(normed[...], wg[...], preferred_element_type=jnp.float32)
    out[...] = silu_halved(part * 0.5)


def attend_kernel(offsets, count_q, ids, mask, *rest):
    count_kv = len(offsets)
    queries = rest[:count_q]
    pairs = rest[count_q:count_q + count_kv]
    outs = rest[count_q + count_kv:count_q + count_kv + count_q]
    live_kv, all_q, all_out = rest[count_q + count_kv + count_q:]
    core, z = ids[1], ids[2]
    blocks = mask.shape[1]
    cap, wide = queries[0].shape
    taken = jnp.int32(0)
    for offset, pair in zip(offsets, pairs):
        there = z + offset
        inside = (there >= 0) & (there < blocks // 2)
        there = jnp.clip(there, 0, blocks // 2 - 1)
        for b in range(2):
            side = core if b == 0 else 1 - core
            live = inside & (mask[0, 2 * there + side] > 0)

            def take(pair=pair, b=b, taken=taken):
                at = pl.multiple_of(taken * BLK, BLK)
                live_kv[pl.ds(at, BLK), :] = pair[b * BLK:(b + 1) * BLK, :]

            pl.when(live)(take)
            taken = jnp.minimum(taken + live.astype(jnp.int32), blocks // 2 - 1)
    for i, q in enumerate(queries):
        all_q[i * cap:(i + 1) * cap, :] = q[...]
    scale = 0.5 * HEAD ** (-0.5)
    total = count_q * cap
    tile = 256 if total % 256 == 0 else cap
    for head in range(wide // HEAD):
        cols = slice(head * HEAD, (head + 1) * HEAD)
        keys = live_kv[:, cols]
        values = live_kv[:, wide + head * HEAD:wide + (head + 1) * HEAD]
        for first in range(0, total, tile):
            scores = lax.dot_general(
                all_q[first:first + tile, cols], keys, (((1,), (1,)), ((), ())),
                preferred_element_type=jnp.float32,
            )
            weight = silu_halved(scores * scale).astype(jnp.bfloat16)
            got = jnp.dot(weight, values, preferred_element_type=jnp.float32)
            all_out[first:first + tile, cols] = got.astype(jnp.bfloat16)
    for i, out in enumerate(outs):
        out[...] = all_out[i * cap:(i + 1) * cap, :]


def finish_kernel(chunks, cap, ids, feat, user, gate, gain, w_out, *rest):
    parts, out, back, attended = rest[:-3], rest[-3], rest[-2], rest[-1]
    me, core = ids[0], ids[1]
    rows, width = feat.shape
    half = width // 2
    wide = half // chunks
    users = rows * 2 // cap
    slot = slots_of(user[...], me, cap)
    places = lax.broadcasted_iota(jnp.int32, (rows, users * cap), 1).astype(jnp.float32)
    pick = (places == slot).astype(jnp.bfloat16)
    for swap in range(2):
        side = core if swap == 0 else 1 - core
        for chunk in range(chunks):
            for d in range(users):
                back[d * cap:(d + 1) * cap, :] = parts[(chunk * 2 + swap) * users + d][...]
            got = jnp.dot(pick, back[...], preferred_element_type=jnp.float32)
            at = pl.multiple_of(side * half + chunk * wide, 128)
            attended[:, pl.ds(at, wide)] = got
    mixed = (centred_norm(attended[...]) * gain[...] * gate[...]).astype(jnp.bfloat16)
    grown = jnp.dot(mixed, w_out[...], preferred_element_type=jnp.float32)
    out[...] = (feat[...].astype(jnp.float32) + grown).astype(jnp.bfloat16)


SMEM = pl.BlockSpec(memory_space=pltpu.SMEM)
VMEM = pl.BlockSpec(memory_space=pltpu.VMEM)


def call(kernel, name, in_specs, out_shape, scratch, flops, *args):
    moved = sum(a.size * a.dtype.itemsize for a in args)
    return pl.pallas_call(
        kernel,
        name=name,
        in_specs=in_specs,
        out_specs=jax.tree.map(lambda s: VMEM, out_shape),
        out_shape=out_shape,
        scratch_shapes=scratch,
        cost_estimate=pl.CostEstimate(flops=flops, bytes_accessed=moved, transcendentals=0),
        compiler_params=pltpu.CompilerParams(vmem_limit_bytes=VMEM_LIMIT),
    )(*args)


def on_device(cand_feat, cand_user, hist_kv, hist_mask, gain_in, w_uq, gain_attn, w_out):
    users = lax.axis_size("users")
    ctx = lax.axis_size("ctx")
    chips = ctx // 2
    rows, width = cand_feat.shape
    cap = 2 * rows // users
    half = width // 2
    wide = half // CHUNKS
    me = lax.axis_index("users")
    place = lax.axis_index("ctx")
    ids = jnp.stack([me, place % 2, place // 2]).astype(jnp.int32)
    bf16 = jnp.bfloat16

    def shape(*dims, dtype=bf16):
        return jax.ShapeDtypeStruct(dims, dtype)

    halves = call(
        functools.partial(kv_split_kernel, CHUNKS), "kv_split", [SMEM, VMEM],
        [shape(BLK, 2 * wide)] * (2 * CHUNKS), [], 0, ids, hist_kv[0, 0],
    )
    core_swap = [(c, c ^ 1) for c in range(ctx)]
    pairs = []
    for chunk in range(CHUNKS):
        other = lax.ppermute(halves[2 * chunk + 1], "ctx", core_swap)
        pairs.append(jnp.concatenate([halves[2 * chunk], other], axis=0))

    def along(value, step, sign):
        moves = []
        for c in range(ctx):
            z = c // 2
            goal = z + sign
            origin = z - sign * (step - 1)
            if 0 <= goal < chips and 0 <= origin < chips:
                moves.append((c, c + 2 * sign))
        return lax.ppermute(value, "ctx", moves)

    def route(value, d, k):
        moves = [(u * ctx + c, (u ^ d) * ctx + (c ^ k)) for u in range(users) for c in range(ctx)]
        return lax.ppermute(value, ("users", "ctx"), moves)

    def exchange(values):
        got = []
        for k in range(2):
            for d in range(users):
                value = values[k * users + d]
                got.append(value if k == 0 and d == 0 else route(value, d, k))
        return got

    normed, *queries = pl.pallas_call(
        functools.partial(query_kernel, CHUNKS, cap),
        name="query",
        grid=(1,),
        in_specs=[
            SMEM,
            pl.BlockSpec((rows, width), lambda i: (0, 0)),
            pl.BlockSpec((rows, 1), lambda i: (0, 0)),
            pl.BlockSpec((1, width), lambda i: (0, 0)),
            pl.BlockSpec((width, width), lambda i: (0, 1)),
        ],
        out_specs=[pl.BlockSpec((rows, width), lambda i: (0, 0))]
        + [pl.BlockSpec((cap, wide), lambda i: (0, 0))] * (CHUNKS * 2 * users),
        out_shape=[shape(rows, width)] + [shape(cap, wide)] * (CHUNKS * 2 * users),
        scratch_shapes=[pltpu.VMEM((2, rows, half), bf16)],
        cost_estimate=pl.CostEstimate(
            flops=4 * rows * width * width, bytes_accessed=2 * width * width, transcendentals=0
        ),
        compiler_params=pltpu.CompilerParams(vmem_limit_bytes=VMEM_LIMIT),
    )(ids, cand_feat, cand_user, gain_in, w_uq[0])

    per_chunk = 2 * users
    arrived = [
        exchange(queries[chunk * per_chunk:(chunk + 1) * per_chunk]) for chunk in range(CHUNKS)
    ]
    offsets = [0]
    for step in range(1, chips):
        offsets += [-step, step]
    gathered = []
    for chunk in range(CHUNKS):
        right = left = pairs[chunk]
        held = [pairs[chunk]]
        for step in range(1, chips):
            right = along(right, step, 1)
            left = along(left, step, -1)
            held += [right, left]
        gathered.append(held)

    gate = pl.pallas_call(
        gate_kernel,
        name="gate",
        grid=(1,),
        in_specs=[
            pl.BlockSpec((rows, width), lambda i: (0, 0)),
            pl.BlockSpec((width, width), lambda i: (0, 0)),
        ],
        out_specs=pl.BlockSpec((rows, width), lambda i: (0, 0)),
        out_shape=shape(rows, width, dtype=jnp.float32),
        cost_estimate=pl.CostEstimate(
            flops=2 * rows * width * width, bytes_accessed=2 * width * width, transcendentals=0
        ),
        compiler_params=pltpu.CompilerParams(vmem_limit_bytes=VMEM_LIMIT),
    )(normed, w_uq[0])

    live_rows = hist_mask.shape[1] // 2 * BLK
    returned = []
    for chunk in range(CHUNKS):
        scored = call(
            functools.partial(attend_kernel, tuple(offsets), per_chunk), "attend",
            [SMEM, SMEM] + [VMEM] * (per_chunk + len(offsets)),
            [shape(cap, wide)] * per_chunk,
            [
                pltpu.VMEM((live_rows, 2 * wide), bf16),
                pltpu.VMEM((per_chunk * cap, wide), bf16),
                pltpu.VMEM((per_chunk * cap, wide), bf16),
            ],
            8 * per_chunk * cap * live_rows * wide,
            ids, hist_mask, *arrived[chunk], *gathered[chunk],
        )
        returned += exchange(scored)

    return call(
        functools.partial(finish_kernel, CHUNKS, cap), "finish",
        [SMEM] + [VMEM] * (5 + len(returned)),
        shape(rows, width),
        [pltpu.VMEM((users * cap, wide), bf16), pltpu.VMEM((rows, width), jnp.float32)],
        4 * rows * width * width,
        ids, cand_feat, cand_user, gate, gain_attn, w_out[0], *returned,
    )


def solution(mesh):
    in_specs = (
        P(("users", "ctx"), None),
        P(("users", "ctx"), None),
        P(None, "users", "ctx", None),
        P("users", None),
        P(),
        P(),
        P(),
        P(),
    )
    out_specs = P(("users", "ctx"), None)
    return jax.shard_map(
        on_device, mesh=mesh, in_specs=in_specs, out_specs=out_specs, check_vma=False
    )
```

```python
import functools

import jax
import jax.numpy as jnp
from jax import lax
from jax.experimental import pallas as pl
from jax.experimental.pallas import tpu as pltpu
from jax.sharding import PartitionSpec as P

BLK = 128
HEAD = 128
CHUNKS = 2
VMEM_LIMIT = 32 * 1024 * 1024


def silu_halved(t):
    return t + t * jnp.tanh(t)


def centred_norm(x):
    middle = jnp.mean(x, axis=-1, keepdims=True)
    shifted = x - middle
    spread = jnp.mean(shifted * shifted, axis=-1, keepdims=True)
    return shifted * lax.rsqrt(spread + 1e-05)


def slots_of(user, me, cap, users):
    rows = user.shape[1]
    rel = user ^ me
    places = max(8, users)
    one_hot = rel == lax.broadcasted_iota(jnp.int32, (places, rows), 0)
    one_hot = one_hot.astype(jnp.float32)
    first = lax.broadcasted_iota(jnp.int32, (rows, rows), 0)
    second = lax.broadcasted_iota(jnp.int32, (rows, rows), 1)
    earlier = (first < second).astype(jnp.bfloat16)
    rank = jnp.dot(one_hot.astype(jnp.bfloat16), earlier, preferred_element_type=jnp.float32)
    rank = jnp.sum(rank * one_hot, axis=0, keepdims=True)
    return rel.astype(jnp.float32) * cap + rank


def kv_split_kernel(chunks, kv, *outs):
    half = kv.shape[1] // 2
    wide = half // chunks
    for chunk in range(chunks):
        for part in range(2):
            outs[chunk][:, part * wide:(part + 1) * wide] = kv[
                :, part * half + chunk * wide:part * half + (chunk + 1) * wide
            ]


def query_kernel(cap, users, ids, feat, user, gain, wq, normed_out, *outs):
    rows, width = feat.shape
    normed = (centred_norm(feat[...].astype(jnp.float32)) * gain[...]).astype(jnp.bfloat16)
    normed_out[...] = normed
    slot = slots_of(user[...], ids[0], cap, users)
    places = lax.broadcasted_iota(jnp.int32, (users * cap, rows), 0).astype(jnp.float32)
    pick = (places == slot).astype(jnp.bfloat16)
    part = jnp.dot(normed, wq[...], preferred_element_type=jnp.float32)
    query = silu_halved(part * 0.5).astype(jnp.bfloat16)
    sent = jnp.dot(pick, query, preferred_element_type=jnp.float32).astype(jnp.bfloat16)
    for d in range(users):
        outs[d][...] = sent[d * cap:(d + 1) * cap, :]


def gate_kernel(cap, users, ids, normed, user, wg, gate, pick):
    rows = user.shape[1]
    part = jnp.dot(normed[...], wg[...], preferred_element_type=jnp.float32)
    gate[...] = silu_halved(part * 0.5)
    slot = slots_of(user[...], ids[0], cap, users)
    slot = jnp.transpose(jnp.broadcast_to(slot, (128, rows)))[:, 0:1]
    places = lax.broadcasted_iota(jnp.int32, (rows, users * cap), 1).astype(jnp.float32)
    pick[...] = (places == slot).astype(jnp.bfloat16)


def attend_kernel(users, chips, ids, mask, *rest):
    queries = rest[:users]
    blocks = rest[users:users + 2 * chips]
    outs, (live_kv, all_q) = rest[-2 - users:-2], rest[-2:]
    core, z = ids[1], ids[2]
    cap, wide = queries[0].shape
    taken = jnp.int32(0)
    for d in range(chips):
        for swap in range(2):
            live = mask[0, 2 * (z ^ d) + (core ^ swap)] > 0

            def take(block=blocks[2 * d + swap], taken=taken):
                at = pl.multiple_of(taken * BLK, BLK)
                live_kv[pl.ds(at, BLK), :] = block[...]

            pl.when(live)(take)
            taken = jnp.minimum(taken + live.astype(jnp.int32), chips - 1)
    for i, q in enumerate(queries):
        all_q[i * cap:(i + 1) * cap, :] = q[...]
    scale = 0.5 * HEAD ** (-0.5)
    for head in range(wide // HEAD):
        cols = slice(head * HEAD, (head + 1) * HEAD)
        keys = live_kv[:, cols]
        values = live_kv[:, wide + head * HEAD:wide + (head + 1) * HEAD]
        scores = lax.dot_general(
            all_q[:, cols], keys, (((1,), (1,)), ((), ())), preferred_element_type=jnp.float32
        )
        weight = silu_halved(scores * scale).astype(jnp.bfloat16)
        got = jnp.dot(weight, values, preferred_element_type=jnp.float32).astype(jnp.bfloat16)
        for i, out in enumerate(outs):
            out[:, cols] = got[i * cap:(i + 1) * cap, :]


def finish_kernel(users, feat, gate, pick, gain, w_out, *rest):
    parts, out, back = rest[:-2], rest[-2], rest[-1]
    cap, wide = parts[0].shape
    for i, part in enumerate(parts):
        chunk, d = i // users, i % users
        back[d * cap:(d + 1) * cap, chunk * wide:(chunk + 1) * wide] = part[...]
    attended = jnp.dot(pick[...], back[...], preferred_element_type=jnp.float32)
    mixed = (centred_norm(attended) * gain[...] * gate[...]).astype(jnp.bfloat16)
    grown = jnp.dot(mixed, w_out[...], preferred_element_type=jnp.float32)
    out[...] = (feat[...].astype(jnp.float32) + grown).astype(jnp.bfloat16)


SMEM = pl.BlockSpec(memory_space=pltpu.SMEM)
ANY = pl.BlockSpec(memory_space=pl.ANY)


def whole(*dims, at=None):
    return pl.BlockSpec(dims, lambda i: at or (0,) * len(dims))


def call(kernel, name, in_specs, out_shape, scratch, flops, *args):
    moved = sum(a.size * a.dtype.itemsize for a in args)
    return pl.pallas_call(
        kernel,
        name=name,
        grid=(1,),
        in_specs=in_specs,
        out_specs=[whole(*s.shape) for s in out_shape],
        out_shape=out_shape,
        scratch_shapes=scratch,
        cost_estimate=pl.CostEstimate(flops=flops, bytes_accessed=moved, transcendentals=0),
        compiler_params=pltpu.CompilerParams(vmem_limit_bytes=VMEM_LIMIT),
    )(*args)


def on_device(cand_feat, cand_user, hist_kv, hist_mask, gain_in, w_uq, gain_attn, w_out):
    users = lax.axis_size("users")
    ctx = lax.axis_size("ctx")
    chips = ctx // 2
    rows, width = cand_feat.shape
    cap = 2 * rows // users
    wide = width // CHUNKS
    me = lax.axis_index("users")
    place = lax.axis_index("ctx")
    ids = jnp.stack([me, place % 2, place // 2]).astype(jnp.int32)
    bf16 = jnp.bfloat16
    user_row = cand_user.reshape(1, rows)

    def shape(*dims, dtype=bf16):
        return jax.ShapeDtypeStruct(dims, dtype)

    def over_z(value, d):
        return lax.ppermute(value, "ctx", [(c, c ^ (2 * d)) for c in range(ctx)])

    def over_cores(value):
        return lax.ppermute(value, "ctx", [(c, c ^ 1) for c in range(ctx)])

    def over_users(values):
        return [values[0]] + [
            lax.ppermute(values[d], "users", [(u, u ^ d) for u in range(users)])
            for d in range(1, users)
        ]

    kv = hist_kv[0, 0]
    split = call(
        functools.partial(kv_split_kernel, CHUNKS), "kv_split", [whole(*kv.shape)],
        [shape(BLK, 2 * wide)] * CHUNKS, [], 0, kv,
    )
    gathered = []
    for own in split:
        held = {0: own}
        for d in [3, 1, 2] + list(range(4, chips)):
            held[d] = over_z(held[3], 1) if d == 2 else over_z(own, d)
        blocks = []
        for d in range(chips):
            blocks += [held[d], over_cores(held[d])]
        gathered.append(blocks)

    normed, *queries = call(
        functools.partial(query_kernel, cap, users), "query",
        [SMEM, whole(rows, width), whole(1, rows), whole(1, width), whole(width, width, at=(0, 1))],
        [shape(rows, width)] + [shape(cap, width)] * users,
        [], 4 * rows * width * width,
        ids, cand_feat, user_row, gain_in, w_uq[0],
    )
    arrived = over_users(queries)

    gate, pick = call(
        functools.partial(gate_kernel, cap, users), "gate",
        [SMEM, whole(rows, width), whole(1, rows), whole(width, width)],
        [shape(rows, width, dtype=jnp.float32), shape(rows, users * cap)],
        [], 2 * rows * width * width,
        ids, normed, user_row, w_uq[0],
    )

    returned = []
    for chunk in range(CHUNKS):
        scored = call(
            functools.partial(attend_kernel, users, chips), "attend",
            [SMEM, SMEM]
            + [whole(cap, wide, at=(0, chunk))] * users
            + [whole(BLK, 2 * wide)] * (2 * chips)
            + [ANY],
            [shape(cap, wide)] * users,
            [pltpu.VMEM((chips * BLK, 2 * wide), bf16), pltpu.VMEM((users * cap, wide), bf16)],
            8 * users * cap * chips * BLK * wide,
            ids, hist_mask, *arrived, *gathered[chunk], gate,
        )
        returned += over_users(scored)

    return call(
        functools.partial(finish_kernel, users), "finish",
        [
            whole(rows, width), whole(rows, width), whole(rows, users * cap), whole(1, width),
            whole(width, width),
        ]
        + [whole(cap, wide)] * len(returned),
        [shape(rows, width)],
        [pltpu.VMEM((users * cap, width), bf16)],
        4 * rows * width * width,
        cand_feat, gate, pick, gain_attn, w_out[0], *returned,
    )[0]


def solution(mesh):
    in_specs = (
        P(("users", "ctx"), None),
        P(("users", "ctx"), None),
        P(None, "users", "ctx", None),
        P("users", None),
        P(),
        P(),
        P(),
        P(),
    )
    out_specs = P(("users", "ctx"), None)
    return jax.shard_map(
        on_device, mesh=mesh, in_specs=in_specs, out_specs=out_specs, check_vma=False
    )
```

```python
import functools

import jax
import jax.numpy as jnp
from jax import lax
from jax.experimental import pallas as pl
from jax.experimental.pallas import tpu as pltpu
from jax.sharding import PartitionSpec as P

BLK = 128
HEAD = 128
CHUNKS = 2
VMEM_LIMIT = 32 * 1024 * 1024
VMEM_MOST = 60 * 1024 * 1024
HEAVY = 4 * 10**11


def silu_halved(t):
    return t + t * jnp.tanh(t)


def centred_norm(x):
    middle = jnp.mean(x, axis=-1, keepdims=True)
    shifted = x - middle
    spread = jnp.mean(shifted * shifted, axis=-1, keepdims=True)
    return shifted * lax.rsqrt(spread + 1e-05)


def slots_of(user, me, cap, users):
    rows = user.shape[1]
    rel = user ^ me
    places = max(8, users)
    one_hot = rel == lax.broadcasted_iota(jnp.int32, (places, rows), 0)
    one_hot = one_hot.astype(jnp.float32)
    first = lax.broadcasted_iota(jnp.int32, (rows, rows), 0)
    second = lax.broadcasted_iota(jnp.int32, (rows, rows), 1)
    earlier = (first < second).astype(jnp.bfloat16)
    rank = jnp.dot(one_hot.astype(jnp.bfloat16), earlier, preferred_element_type=jnp.float32)
    rank = jnp.sum(rank * one_hot, axis=0, keepdims=True)
    return rel.astype(jnp.float32) * cap + rank


def kv_split_kernel(chunks, kv, *outs):
    half = kv.shape[1] // 2
    wide = half // chunks
    for chunk in range(chunks):
        for part in range(2):
            outs[chunk][:, part * wide:(part + 1) * wide] = kv[
                :, part * half + chunk * wide:part * half + (chunk + 1) * wide
            ]


def query_kernel(cap, users, feat_in, user_in, gain_in, w_in, normed_out, *rest):
    outs, (feat, user, gain, wq, sems) = rest[:users], rest[users:]
    rows, width = feat.shape
    half = width // 2
    copies = [
        pltpu.make_async_copy(feat_in, feat, sems.at[0]),
        pltpu.make_async_copy(user_in, user, sems.at[1]),
        pltpu.make_async_copy(gain_in, gain, sems.at[2]),
    ]
    for side in range(2):
        copies.append(
            pltpu.make_async_copy(
                w_in.at[:, pl.ds(width + side * half, half)], wq.at[side], sems.at[3 + side]
            )
        )
    for copy in copies:
        copy.start()
    copies[1].wait()
    slot = slots_of(user[...], lax.axis_index("users"), cap, users)
    places = lax.broadcasted_iota(jnp.int32, (users * cap, rows), 0).astype(jnp.float32)
    pick = (places == slot).astype(jnp.bfloat16)
    copies[0].wait()
    copies[2].wait()
    normed = (centred_norm(feat[...].astype(jnp.float32)) * gain[...]).astype(jnp.bfloat16)
    normed_out[...] = normed
    for side in range(2):
        copies[3 + side].wait()
        part = jnp.dot(normed, wq[side], preferred_element_type=jnp.float32)
        query = silu_halved(part * 0.5).astype(jnp.bfloat16)
        sent = jnp.dot(pick, query, preferred_element_type=jnp.float32).astype(jnp.bfloat16)
        for d in range(users):
            outs[d][:, side * half:(side + 1) * half] = sent[d * cap:(d + 1) * cap, :]


def gate_kernel(cap, users, normed_in, user_in, w_in, gate, pick, normed, user, wg, sems):
    rows, width = normed.shape
    half = width // 2
    copies = [
        pltpu.make_async_copy(user_in, user, sems.at[0]),
        pltpu.make_async_copy(normed_in, normed, sems.at[1]),
    ]
    for side in range(2):
        copies.append(
            pltpu.make_async_copy(
                w_in.at[:, pl.ds(side * half, half)], wg.at[side], sems.at[2 + side]
            )
        )
    for copy in copies:
        copy.start()
    copies[0].wait()
    slot = slots_of(user[...], lax.axis_index("users"), cap, users)
    slot = jnp.transpose(jnp.broadcast_to(slot, (128, rows)))[:, 0:1]
    places = lax.broadcasted_iota(jnp.int32, (rows, users * cap), 1).astype(jnp.float32)
    pick[...] = (places == slot).astype(jnp.bfloat16)
    copies[1].wait()
    for side in range(2):
        copies[2 + side].wait()
        part = jnp.dot(normed[...], wg[side], preferred_element_type=jnp.float32)
        gate[:, side * half:(side + 1) * half] = silu_halved(part * 0.5)


def attend_kernel(users, chips, mask, *rest):
    queries = rest[:users]
    blocks = rest[users:users + 2 * chips]
    outs, (live_kv, all_q) = rest[-2 - users:-2], rest[-2:]
    place = lax.axis_index("ctx")
    core, z = place % 2, place // 2
    cap, wide = queries[0].shape
    taken = jnp.int32(0)
    for d in range(chips):
        for swap in range(2):
            live = mask[0, 2 * (z ^ d) + (core ^ swap)] > 0

            def take(block=blocks[2 * d + swap], taken=taken):
                at = pl.multiple_of(taken * BLK, BLK)
                live_kv[pl.ds(at, BLK), :] = block[...]

            pl.when(live)(take)
            taken = jnp.minimum(taken + live.astype(jnp.int32), chips - 1)
    for i, q in enumerate(queries):
        all_q[i * cap:(i + 1) * cap, :] = q[...]
    scale = 0.5 * HEAD ** (-0.5)
    for head in range(wide // HEAD):
        cols = slice(head * HEAD, (head + 1) * HEAD)
        keys = live_kv[:, cols]
        values = live_kv[:, wide + head * HEAD:wide + (head + 1) * HEAD]
        scores = lax.dot_general(
            all_q[:, cols], keys, (((1,), (1,)), ((), ())), preferred_element_type=jnp.float32
        )
        weight = silu_halved(scores * scale).astype(jnp.bfloat16)
        got = jnp.dot(weight, values, preferred_element_type=jnp.float32).astype(jnp.bfloat16)
        for i, out in enumerate(outs):
            out[:, cols] = got[i * cap:(i + 1) * cap, :]


def finish_kernel(users, feat, gate, pick, gain, w_out, *rest):
    parts, out, back = rest[:-2], rest[-2], rest[-1]
    cap, wide = parts[0].shape
    for i, part in enumerate(parts):
        chunk, d = i // users, i % users
        back[d * cap:(d + 1) * cap, chunk * wide:(chunk + 1) * wide] = part[...]
    attended = jnp.dot(pick[...], back[...], preferred_element_type=jnp.float32)
    mixed = (centred_norm(attended) * gain[...] * gate[...]).astype(jnp.bfloat16)
    grown = jnp.dot(mixed, w_out[...], preferred_element_type=jnp.float32)
    out[...] = (feat[...].astype(jnp.float32) + grown).astype(jnp.bfloat16)


SMEM = pl.BlockSpec(memory_space=pltpu.SMEM)
HBM = pl.BlockSpec(memory_space=pltpu.HBM)


def whole(*dims, at=None):
    return pl.BlockSpec(dims, lambda i: at or (0,) * len(dims))


def call(kernel, name, in_specs, out_shape, scratch, flops, *args, vmem=VMEM_LIMIT):
    moved = sum(a.size * a.dtype.itemsize for a in args)
    return pl.pallas_call(
        kernel,
        name=name,
        grid=(1,),
        in_specs=in_specs,
        out_specs=[whole(*s.shape) for s in out_shape],
        out_shape=out_shape,
        scratch_shapes=scratch,
        cost_estimate=pl.CostEstimate(flops=flops, bytes_accessed=moved, transcendentals=0),
        compiler_params=pltpu.CompilerParams(vmem_limit_bytes=vmem),
    )(*args)


def on_device(cand_feat, cand_user, hist_kv, hist_mask, gain_in, w_uq, gain_attn, w_out):
    users = lax.axis_size("users")
    ctx = lax.axis_size("ctx")
    chips = ctx // 2
    rows, width = cand_feat.shape
    cap = 2 * rows // users
    wide = width // CHUNKS
    bf16 = jnp.bfloat16
    user_row = cand_user.reshape(1, rows)

    def shape(*dims, dtype=bf16):
        return jax.ShapeDtypeStruct(dims, dtype)

    def over_z(value, d):
        return lax.ppermute(value, "ctx", [(c, c ^ (2 * d)) for c in range(ctx)])

    def over_cores(value):
        return lax.ppermute(value, "ctx", [(c, c ^ 1) for c in range(ctx)])

    def over_users(values):
        return [values[0]] + [
            lax.ppermute(values[d], "users", [(u, u ^ d) for u in range(users)])
            for d in range(1, users)
        ]

    def after(value, *others):
        return lax.optimization_barrier((value, *others))[0]

    kv = hist_kv[0, 0]
    split = call(
        functools.partial(kv_split_kernel, CHUNKS), "kv_split", [whole(*kv.shape)],
        [shape(BLK, 2 * wide)] * CHUNKS, [], 0, kv,
    )

    normed, *queries = call(
        functools.partial(query_kernel, cap, users), "query",
        [HBM] * 4,
        [shape(rows, width)] + [shape(cap, width)] * users,
        [
            pltpu.VMEM((rows, width), bf16),
            pltpu.VMEM((1, rows), jnp.int32),
            pltpu.VMEM((1, width), jnp.float32),
            pltpu.VMEM((2, width, width // 2), bf16),
            pltpu.SemaphoreType.DMA((5,)),
        ],
        HEAVY,
        after(cand_feat, split[0]), user_row, gain_in, w_uq[0], vmem=VMEM_MOST,
    )
    arrived = over_users(queries)

    gate, pick = call(
        functools.partial(gate_kernel, cap, users), "gate",
        [HBM] * 3,
        [shape(rows, width, dtype=jnp.float32), shape(rows, users * cap)],
        [
            pltpu.VMEM((rows, width), bf16),
            pltpu.VMEM((1, rows), jnp.int32),
            pltpu.VMEM((2, width, width // 2), bf16),
            pltpu.SemaphoreType.DMA((4,)),
        ],
        HEAVY,
        normed, user_row, w_uq[0], vmem=VMEM_MOST,
    )

    returned, earlier = [], None
    for chunk in range(CHUNKS):
        held = {0: split[chunk]}
        far, near = split[chunk], split[chunk]
        if chunk:
            far = after(far, earlier[3], gate)
            near = after(near, earlier[1], gate)
        for d in [3, 1, 2] + list(range(4, chips)):
            held[d] = over_z(held[3], 1) if d == 2 else over_z(near if d == 1 else far, d)
        blocks = []
        for d in range(chips):
            if chunk == 0:
                ready = arrived[1:2] if d != 2 else []
            else:
                ready = returned[-users + 1:] if d in (1, 2) else []
            blocks += [held[d], over_cores(after(held[d], *ready) if ready else held[d])]
        earlier = held
        scored = call(
            functools.partial(attend_kernel, users, chips), "attend",
            [SMEM] + [whole(cap, wide, at=(0, chunk))] * users + [whole(BLK, 2 * wide)] * (2 * chips),
            [shape(cap, wide)] * users,
            [pltpu.VMEM((chips * BLK, 2 * wide), bf16), pltpu.VMEM((users * cap, wide), bf16)],
            8 * users * cap * chips * BLK * wide,
            hist_mask, *arrived, *blocks,
        )
        returned += over_users(scored)

    return call(
        functools.partial(finish_kernel, users), "finish",
        [
            whole(rows, width), whole(rows, width), whole(rows, users * cap), whole(1, width),
            whole(width, width),
        ]
        + [whole(cap, wide)] * len(returned),
        [shape(rows, width)],
        [pltpu.VMEM((users * cap, width), bf16)],
        4 * rows * width * width,
        cand_feat, gate, pick, gain_attn, w_out[0], *returned,
    )[0]


def solution(mesh):
    in_specs = (
        P(("users", "ctx"), None),
        P(("users", "ctx"), None),
        P(None, "users", "ctx", None),
        P("users", None),
        P(),
        P(),
        P(),
        P(),
    )
    out_specs = P(("users", "ctx"), None)
    return jax.shard_map(
        on_device, mesh=mesh, in_specs=in_specs, out_specs=out_specs, check_vma=False
    )
```

```python
import functools

import jax
import jax.numpy as jnp
from jax import lax
from jax.experimental import pallas as pl
from jax.experimental.pallas import tpu as pltpu
from jax.sharding import PartitionSpec as P

BLK = 128
HEAD = 128
OPTS = {'chunks': [4, 4], 'order': 0, 'qs': 0, 'cq': 10000000000, 'cg': 0, 'ca': 1000000000, 'cf': 10000000000, 'm1': [], 'a1': [], 'g': ['m0'], 's0': [['qx'], ['g', 'qy'], ['g'], []], 's1': [['s', 'rx'], ['ry'], [], []]}
CHUNKS = OPTS['chunks']
SIDES = 4
VMEM_LIMIT = 32 * 1024 * 1024
VMEM_MOST = 60 * 1024 * 1024
HEAVY = 4 * 10**11


def silu_halved(t):
    return t + t * jnp.tanh(t)


def centred_norm(x):
    middle = jnp.mean(x, axis=-1, keepdims=True)
    shifted = x - middle
    spread = jnp.mean(shifted * shifted, axis=-1, keepdims=True)
    return shifted * lax.rsqrt(spread + 1e-05)


def slots_of(user, me, cap, users):
    rows = user.shape[1]
    rel = user ^ me
    places = max(8, users)
    one_hot = rel == lax.broadcasted_iota(jnp.int32, (places, rows), 0)
    one_hot = one_hot.astype(jnp.float32)
    first = lax.broadcasted_iota(jnp.int32, (rows, rows), 0)
    second = lax.broadcasted_iota(jnp.int32, (rows, rows), 1)
    earlier = (first < second).astype(jnp.bfloat16)
    rank = jnp.dot(one_hot.astype(jnp.bfloat16), earlier, preferred_element_type=jnp.float32)
    rank = jnp.sum(rank * one_hot, axis=0, keepdims=True)
    return rel.astype(jnp.float32) * cap + rank


def kv_split_kernel(kv, *rest):
    outs, sems = rest[:-1], rest[-1]
    half = kv.shape[1] // 2
    copies, first = [], 0
    for out in outs:
        wide = out.shape[1] // 2
        for part in range(2):
            copies.append(
                pltpu.make_async_copy(
                    kv.at[:, pl.ds(part * half + first, wide)],
                    out.at[:, pl.ds(part * wide, wide)],
                    sems.at[len(copies)],
                )
            )
        first += wide
    for copy in copies:
        copy.start()
    for copy in copies:
        copy.wait()


def query_kernel(cap, users, feat_in, user_in, gain_in, w_in, *rest):
    outs, (feat, user, gain, wq, sent, sems, out_sems) = rest[:users], rest[users:]
    rows, width = feat.shape
    sides, _, part_width = wq.shape
    copies = [
        pltpu.make_async_copy(user_in, user, sems.at[0]),
        pltpu.make_async_copy(feat_in, feat, sems.at[1]),
        pltpu.make_async_copy(gain_in, gain, sems.at[2]),
    ]
    for side in range(sides):
        copies.append(
            pltpu.make_async_copy(
                w_in.at[:, pl.ds(width + side * part_width, part_width)],
                wq.at[side],
                sems.at[3 + side],
            )
        )
    for copy in copies:
        copy.start()
    copies[0].wait()
    slot = slots_of(user[...], lax.axis_index("users"), cap, users)
    places = lax.broadcasted_iota(jnp.int32, (users * cap, rows), 0).astype(jnp.float32)
    pick = (places == slot).astype(jnp.bfloat16)
    copies[1].wait()
    copies[2].wait()
    normed = (centred_norm(feat[...].astype(jnp.float32)) * gain[...]).astype(jnp.bfloat16)
    writes = []
    for side in range(sides):
        copies[3 + side].wait()
        cols = slice(side * part_width, (side + 1) * part_width)
        part = jnp.dot(normed, wq[side], preferred_element_type=jnp.float32)
        query = silu_halved(part * 0.5).astype(jnp.bfloat16)
        sent[:, cols] = jnp.dot(pick, query, preferred_element_type=jnp.float32).astype(
            jnp.bfloat16
        )
        for d in range(users):
            write = pltpu.make_async_copy(
                sent.at[pl.ds(d * cap, cap), pl.ds(side * part_width, part_width)],
                outs[d].at[:, pl.ds(side * part_width, part_width)],
                out_sems.at[side * users + d],
            )
            write.start()
            writes.append(write)
    for write in writes:
        write.wait()


def gate_kernel(cap, users, feat_in, user_in, gain_in, w_in, gate, pick, feat, user, gain, wg, sems):
    rows, width = feat.shape
    sides, _, part_width = wg.shape
    copies = [
        pltpu.make_async_copy(user_in, user, sems.at[0]),
        pltpu.make_async_copy(feat_in, feat, sems.at[1]),
        pltpu.make_async_copy(gain_in, gain, sems.at[2]),
    ]
    for side in range(sides):
        copies.append(
            pltpu.make_async_copy(
                w_in.at[:, pl.ds(side * part_width, part_width)], wg.at[side], sems.at[3 + side]
            )
        )
    for copy in copies:
        copy.start()
    copies[0].wait()
    slot = slots_of(user[...], lax.axis_index("users"), cap, users)
    slot = jnp.transpose(jnp.broadcast_to(slot, (128, rows)))[:, 0:1]
    places = lax.broadcasted_iota(jnp.int32, (rows, users * cap), 1).astype(jnp.float32)
    pick[...] = (places == slot).astype(jnp.bfloat16)
    copies[1].wait()
    copies[2].wait()
    normed = (centred_norm(feat[...].astype(jnp.float32)) * gain[...]).astype(jnp.bfloat16)
    for side in range(sides):
        copies[3 + side].wait()
        part = jnp.dot(normed, wg[side], preferred_element_type=jnp.float32)
        gate[:, side * part_width:(side + 1) * part_width] = silu_halved(part * 0.5)


def attend_kernel(users, chips, first, mask, *rest):
    queries = rest[:users]
    blocks = rest[users:users + 2 * chips]
    outs, (live_kv, all_q) = rest[-2 - users:-2], rest[-2:]
    place = lax.axis_index("ctx")
    core, z = place % 2, place // 2
    cap, wide = outs[0].shape
    taken = jnp.int32(0)
    for d in range(chips):
        for swap in range(2):
            live = mask[0, 2 * (z ^ d) + (core ^ swap)] > 0

            def take(block=blocks[2 * d + swap], taken=taken):
                at = pl.multiple_of(taken * BLK, BLK)
                live_kv[pl.ds(at, BLK), :] = block[...]

            pl.when(live)(take)
            taken = jnp.minimum(taken + live.astype(jnp.int32), chips - 1)
    for i, q in enumerate(queries):
        all_q[i * cap:(i + 1) * cap, :] = q[:, first:first + wide]
    scale = 0.5 * HEAD ** (-0.5)
    for head in range(wide // HEAD):
        cols = slice(head * HEAD, (head + 1) * HEAD)
        keys = live_kv[:, cols]
        values = live_kv[:, wide + head * HEAD:wide + (head + 1) * HEAD]
        scores = lax.dot_general(
            all_q[:, cols], keys, (((1,), (1,)), ((), ())), preferred_element_type=jnp.float32
        )
        weight = silu_halved(scores * scale).astype(jnp.bfloat16)
        got = jnp.dot(weight, values, preferred_element_type=jnp.float32).astype(jnp.bfloat16)
        for i, out in enumerate(outs):
            out[:, cols] = got[i * cap:(i + 1) * cap, :]


def finish_kernel(users, feat, gate, pick, gain, w_out, *rest):
    parts, out, back = rest[:-2], rest[-2], rest[-1]
    first = 0
    for chunk in range(len(parts) // users):
        cap, wide = parts[chunk * users].shape
        for d in range(users):
            part = parts[chunk * users + d]
            back[d * cap:(d + 1) * cap, first:first + wide] = part[...]
        first += wide
    attended = jnp.dot(pick[...], back[...], preferred_element_type=jnp.float32)
    mixed = (centred_norm(attended) * gain[...] * gate[...]).astype(jnp.bfloat16)
    grown = jnp.dot(mixed, w_out[...], preferred_element_type=jnp.float32)
    out[...] = (feat[...].astype(jnp.float32) + grown).astype(jnp.bfloat16)


SMEM = pl.BlockSpec(memory_space=pltpu.SMEM)
HBM = pl.BlockSpec(memory_space=pltpu.HBM)


def whole(*dims, at=None):
    return pl.BlockSpec(dims, lambda i: at or (0,) * len(dims))


def call(kernel, name, in_specs, out_shape, scratch, flops, *args, vmem=VMEM_LIMIT):
    moved = sum(a.size * a.dtype.itemsize for a in args)
    return pl.pallas_call(
        kernel,
        name=name,
        grid=(1,),
        in_specs=in_specs,
        out_specs=[whole(*s.shape) for s in out_shape],
        out_shape=out_shape,
        scratch_shapes=scratch,
        cost_estimate=pl.CostEstimate(flops=flops, bytes_accessed=moved if flops else 0, transcendentals=0),
        compiler_params=pltpu.CompilerParams(vmem_limit_bytes=vmem),
    )(*args)


def on_device(cand_feat, cand_user, hist_kv, hist_mask, gain_in, w_uq, gain_attn, w_out):
    users = lax.axis_size("users")
    ctx = lax.axis_size("ctx")
    chips = ctx // 2
    rows, width = cand_feat.shape
    cap = 2 * rows // users
    wides = [heads * HEAD for heads in CHUNKS]
    bf16 = jnp.bfloat16
    user_row = cand_user.reshape(1, rows)

    def shape(*dims, dtype=bf16):
        return jax.ShapeDtypeStruct(dims, dtype)

    def over_z(value, d):
        return lax.ppermute(value, "ctx", [(c, c ^ (2 * d)) for c in range(ctx)])

    def over_cores(value):
        return lax.ppermute(value, "ctx", [(c, c ^ 1) for c in range(ctx)])

    def to_user(value, d):
        return lax.ppermute(value, "users", [(u, u ^ d) for u in range(users)])

    def after(value, *others):
        return lax.optimization_barrier((value, *others))[0]

    def over_users(values):
        if OPTS['order'] == 0:
            got = [to_user(values[d], d) for d in range(users - 1, 0, -1)]
            return [values[0]] + got[::-1]
        return [values[0]] + [to_user(values[d], d) for d in range(1, users)]

    kv = hist_kv[0, 0]
    split = pl.pallas_call(
        kv_split_kernel,
        name="kv_split",
        in_specs=[HBM],
        out_specs=[HBM] * len(wides),
        out_shape=[shape(BLK, 2 * wide) for wide in wides],
        scratch_shapes=[pltpu.SemaphoreType.DMA((2 * len(wides),))],
        cost_estimate=pl.CostEstimate(flops=0, bytes_accessed=4 * kv.size, transcendentals=0),
        compiler_params=pltpu.CompilerParams(vmem_limit_bytes=VMEM_MOST),
    )(kv)

    operands = [
        pltpu.VMEM((rows, width), bf16),
        pltpu.VMEM((1, rows), jnp.int32),
        pltpu.VMEM((1, width), jnp.float32),
        pltpu.VMEM((SIDES, width, width // SIDES), bf16),
    ]
    queries = pl.pallas_call(
        functools.partial(query_kernel, cap, users),
        name="query",
        in_specs=[HBM] * 4,
        out_specs=[HBM] * users,
        out_shape=[shape(cap, width)] * users,
        scratch_shapes=operands + [
            pltpu.VMEM((users * cap, width), bf16),
            pltpu.SemaphoreType.DMA((3 + SIDES,)),
            pltpu.SemaphoreType.DMA((SIDES * users,)),
        ],
        cost_estimate=pl.CostEstimate(flops=OPTS['cq'], bytes_accessed=0, transcendentals=0),
        compiler_params=pltpu.CompilerParams(vmem_limit_bytes=VMEM_MOST),
    )((after(cand_feat, split[0]) if OPTS['qs'] else cand_feat), user_row, gain_in, w_uq[0])
    arrived = over_users(queries)

    returned, first, env = [], 0, {}
    env.update({'qx': arrived[1], 'qy': arrived[2], 'qd': arrived[3], 'q': queries[0]})

    def gated(value, keys):
        ready = [env[k] for k in keys]
        return after(value, *ready) if ready else value

    for chunk, wide in enumerate(wides):
        held = {0: split[chunk]}
        far = near = split[chunk]
        if chunk:
            c = str(chunk - 1)
            far = gated(far, [k + c if k in 'maf' else k for k in OPTS['m1']])
            near = gated(near, [k + c if k in 'maf' else k for k in OPTS['a1']])
        for d in [3, 1, 2] + list(range(4, chips)):
            held[d] = over_z(held[3], 1) if d == 2 else over_z(near if d == 1 else far, d)
        env.update({'a' + str(chunk): held[1], 'm' + str(chunk): held[3], 'f' + str(chunk): held[2]})
        if chunk == 0:
            gate, pick = call(
                functools.partial(gate_kernel, cap, users), "gate",
                [HBM] * 4,
                [shape(rows, width, dtype=jnp.float32), shape(rows, users * cap)],
                operands + [pltpu.SemaphoreType.DMA((3 + SIDES,))],
                OPTS['cg'],
                gated(cand_feat, ['q'] + OPTS['g']), user_row, gain_in, w_uq[0], vmem=VMEM_MOST,
            )
            env['g'] = gate
        blocks = []
        for d in range(chips):
            if chunk == 0:
                keys = OPTS['s0'][d % 4]
            else:
                keys = OPTS['s1'][d % 4]
            blocks += [held[d], over_cores(gated(held[d], keys))]
        scored = call(
            functools.partial(attend_kernel, users, chips, first), "attend",
            [SMEM] + [whole(cap, width)] * users + [whole(BLK, 2 * wide)] * (2 * chips),
            [shape(cap, wide)] * users,
            [pltpu.VMEM((chips * BLK, 2 * wide), bf16), pltpu.VMEM((users * cap, wide), bf16)],
            OPTS['ca'],
            hist_mask, *arrived, *blocks,
        )
        back = over_users(scored)
        env.update({'s': scored[0], 'rx': back[1], 'ry': back[2], 'rd': back[3]})
        returned += back
        first += wide

    return call(
        functools.partial(finish_kernel, users), "finish",
        [
            whole(rows, width), whole(rows, width), whole(rows, users * cap), whole(1, width),
            whole(width, width),
        ]
        + [whole(*part.shape) for part in returned],
        [shape(rows, width)],
        [pltpu.VMEM((users * cap, width), bf16)],
        OPTS["cf"],
        cand_feat, gate, pick, gain_attn, w_out[0], *returned,
    )[0]


def solution(mesh):
    in_specs = (
        P(("users", "ctx"), None),
        P(("users", "ctx"), None),
        P(None, "users", "ctx", None),
        P("users", None),
        P(),
        P(),
        P(),
        P(),
    )
    out_specs = P(("users", "ctx"), None)
    return jax.shard_map(
        on_device, mesh=mesh, in_specs=in_specs, out_specs=out_specs, check_vma=False
    )
```

```python
import functools

import jax
import jax.numpy as jnp
from jax import lax
from jax.experimental import pallas as pl
from jax.experimental.pallas import tpu as pltpu
from jax.sharding import PartitionSpec as P

BLK = 128
HEAD = 128
OPTS = {'chunks': [4, 4], 'order': 0, 'cq': 400000000000, 'cg': 400000000000, 'ca': 0, 'cf': 0, 'cp': 0, 'cs': 0, 'a': [], 'g': ['a', 'qx'], 'f0': ['g'], 'f1': ['g', 'a'], 'pk': ['f', 'g'], 'p': ['g', 'qx', 'qy', 'f'], 's0': ['p'], 's1': ['s']}
CHUNKS = OPTS['chunks']
SLICES = 2
VMEM_LIMIT = 32 * 1024 * 1024
VMEM_MOST = 60 * 1024 * 1024
HEAVY = 4 * 10**11


def silu_halved(t):
    return t + t * jnp.tanh(t)


def centred_norm(x):
    middle = jnp.mean(x, axis=-1, keepdims=True)
    shifted = x - middle
    spread = jnp.mean(shifted * shifted, axis=-1, keepdims=True)
    return shifted * lax.rsqrt(spread + 1e-05)


def slots_of(user, me, cap, users):
    rows = user.shape[1]
    rel = user ^ me
    places = max(8, users)
    one_hot = rel == lax.broadcasted_iota(jnp.int32, (places, rows), 0)
    one_hot = one_hot.astype(jnp.float32)
    first = lax.broadcasted_iota(jnp.int32, (rows, rows), 0)
    second = lax.broadcasted_iota(jnp.int32, (rows, rows), 1)
    earlier = (first < second).astype(jnp.bfloat16)
    rank = jnp.dot(one_hot.astype(jnp.bfloat16), earlier, preferred_element_type=jnp.float32)
    rank = jnp.sum(rank * one_hot, axis=0, keepdims=True)
    return rel.astype(jnp.float32) * cap + rank


def kv_split_kernel(kv, *outs):
    half = kv.shape[1] // 2
    first = 0
    for out in outs:
        wide = out.shape[1] // 2
        for part in range(2):
            out[:, part * wide:(part + 1) * wide] = kv[
                :, part * half + first:part * half + first + wide
            ]
        first += wide


def load_operands(first_col, feat_in, user_in, gain_in, w_in, feat, user, gain, weights, sems):
    slices, depth, width = weights.shape
    copies = [
        pltpu.make_async_copy(user_in, user, sems.at[0]),
        pltpu.make_async_copy(feat_in, feat, sems.at[1]),
        pltpu.make_async_copy(gain_in, gain, sems.at[2]),
    ]
    for k in range(slices):
        copies.append(
            pltpu.make_async_copy(
                w_in.at[pl.ds(k * depth, depth), pl.ds(first_col, width)],
                weights.at[k],
                sems.at[3 + k],
            )
        )
    for copy in copies:
        copy.start()
    return copies


def project(copies, feat, gain, weights):
    slices, depth, _ = weights.shape
    copies[1].wait()
    copies[2].wait()
    normed = (centred_norm(feat[...].astype(jnp.float32)) * gain[...]).astype(jnp.bfloat16)
    total = None
    for k in range(slices):
        copies[3 + k].wait()
        part = jnp.dot(
            normed[:, k * depth:(k + 1) * depth], weights[k], preferred_element_type=jnp.float32
        )
        total = part if total is None else total + part
    return silu_halved(total * 0.5)


def query_kernel(cap, users, feat_in, user_in, gain_in, w_in, *rest):
    outs, (feat, user, gain, weights, sent, sems, out_sems) = rest[:users], rest[users:]
    rows, width = feat.shape
    copies = load_operands(width, feat_in, user_in, gain_in, w_in, feat, user, gain, weights, sems)
    copies[0].wait()
    slot = slots_of(user[...], lax.axis_index("users"), cap, users)
    places = lax.broadcasted_iota(jnp.int32, (users * cap, rows), 0).astype(jnp.float32)
    pick = (places == slot).astype(jnp.bfloat16)
    query = project(copies, feat, gain, weights).astype(jnp.bfloat16)
    writes = []
    for d in range(users):
        at = slice(d * cap, (d + 1) * cap)
        sent[at, :] = jnp.dot(pick[at, :], query, preferred_element_type=jnp.float32).astype(
            jnp.bfloat16
        )
        writes.append(
            pltpu.make_async_copy(sent.at[pl.ds(d * cap, cap), :], outs[d], out_sems.at[d])
        )
        writes[-1].start()
    for write in writes:
        write.wait()


def gate_kernel(cap, users, feat_in, user_in, gain_in, w_in, gate, pick, feat, user, gain, weights, sems):
    rows, _ = feat.shape
    copies = load_operands(0, feat_in, user_in, gain_in, w_in, feat, user, gain, weights, sems)
    copies[0].wait()
    slot = slots_of(user[...], lax.axis_index("users"), cap, users)
    slot = jnp.transpose(jnp.broadcast_to(slot, (128, rows)))[:, 0:1]
    places = lax.broadcasted_iota(jnp.int32, (rows, users * cap), 1).astype(jnp.float32)
    pick[...] = (places == slot).astype(jnp.bfloat16)
    gate[...] = project(copies, feat, gain, weights)


def early_chips(chips):
    return [d for d in range(chips) if d != 2]


def pack_kernel(chips, mask, *rest):
    blocks, out = rest[:-1], rest[-1]
    place = lax.axis_index("ctx")
    core, z = place % 2, place // 2
    taken = jnp.int32(0)
    for d, block in zip(early_chips(chips), blocks):
        live = mask[0, 2 * (z ^ d) + core] > 0

        def take(block=block, taken=taken):
            at = pl.multiple_of(taken * BLK, BLK)
            out[pl.ds(at, BLK), :] = block[...]

        pl.when(live)(take)
        taken = taken + live.astype(jnp.int32)


def attend_kernel(users, chips, first, mask, *rest):
    queries, packs, lasts = rest[:users], rest[users:users + 2], rest[users + 2:users + 4]
    outs, (all_q, live_kv) = rest[users + 4:2 * users + 4], rest[2 * users + 4:]
    cap, wide = outs[0].shape
    width = packs[0].shape[1] // 2
    place = lax.axis_index("ctx")
    core, z = place % 2, place // 2
    taken = jnp.int32(0)

    def take(live, block, parts, taken):
        def copy():
            at = pl.multiple_of(jnp.minimum(taken, chips - 1) * BLK, BLK)
            for part, cols in enumerate(parts):
                live_kv[pl.ds(at, BLK), part * wide:(part + 1) * wide] = block[:, cols]

        pl.when(live)(copy)
        return taken + live.astype(jnp.int32)

    for swap, pack in enumerate(packs):
        count = jnp.int32(0)
        for d in early_chips(chips):
            count = count + (mask[0, 2 * (z ^ d) + (core ^ swap)] > 0).astype(jnp.int32)
        parts = [slice(part * width + first, part * width + first + wide) for part in range(2)]
        for slot in range(chips - 1):
            taken = take(slot < count, pack.at[slot * BLK:(slot + 1) * BLK, :], parts, taken)
    for swap, last in enumerate(lasts):
        live = mask[0, 2 * (z ^ 2) + (core ^ swap)] > 0
        parts = [slice(part * wide, (part + 1) * wide) for part in range(2)]
        taken = take(live, last, parts, taken)
    for i, q in enumerate(queries):
        all_q[i * cap:(i + 1) * cap, :] = q[:, first:first + wide]
    scale = 0.5 * HEAD ** (-0.5)
    for head in range(wide // HEAD):
        cols = slice(head * HEAD, (head + 1) * HEAD)
        keys = live_kv[:, cols]
        values = live_kv[:, wide + head * HEAD:wide + (head + 1) * HEAD]
        scores = lax.dot_general(
            all_q[:, cols], keys, (((1,), (1,)), ((), ())), preferred_element_type=jnp.float32
        )
        weight = silu_halved(scores * scale).astype(jnp.bfloat16)
        got = jnp.dot(weight, values, preferred_element_type=jnp.float32).astype(jnp.bfloat16)
        for i, out in enumerate(outs):
            out[:, cols] = got[i * cap:(i + 1) * cap, :]


def finish_kernel(users, feat, gate, pick, gain, w_out, *rest):
    parts, out, back = rest[:-2], rest[-2], rest[-1]
    first = 0
    for chunk in range(len(parts) // users):
        cap, wide = parts[chunk * users].shape
        for d in range(users):
            part = parts[chunk * users + d]
            back[d * cap:(d + 1) * cap, first:first + wide] = part[...]
        first += wide
    attended = jnp.dot(pick[...], back[...], preferred_element_type=jnp.float32)
    mixed = (centred_norm(attended) * gain[...] * gate[...]).astype(jnp.bfloat16)
    grown = jnp.dot(mixed, w_out[...], preferred_element_type=jnp.float32)
    out[...] = (feat[...].astype(jnp.float32) + grown).astype(jnp.bfloat16)


SMEM = pl.BlockSpec(memory_space=pltpu.SMEM)
HBM = pl.BlockSpec(memory_space=pltpu.HBM)


def whole(*dims, at=None):
    return pl.BlockSpec(dims, lambda i: at or (0,) * len(dims))


def call(kernel, name, in_specs, out_shape, scratch, flops, *args, vmem=VMEM_LIMIT):
    moved = sum(a.size * a.dtype.itemsize for a in args)
    return pl.pallas_call(
        kernel,
        name=name,
        grid=(1,),
        in_specs=in_specs,
        out_specs=[whole(*s.shape) for s in out_shape],
        out_shape=out_shape,
        scratch_shapes=scratch,
        cost_estimate=pl.CostEstimate(flops=flops, bytes_accessed=moved if flops else 0, transcendentals=0),
        compiler_params=pltpu.CompilerParams(vmem_limit_bytes=vmem),
    )(*args)


def on_device(cand_feat, cand_user, hist_kv, hist_mask, gain_in, w_uq, gain_attn, w_out):
    users = lax.axis_size("users")
    ctx = lax.axis_size("ctx")
    chips = ctx // 2
    rows, width = cand_feat.shape
    cap = 2 * rows // users
    wides = [heads * HEAD for heads in CHUNKS]
    bf16 = jnp.bfloat16
    user_row = cand_user.reshape(1, rows)

    def shape(*dims, dtype=bf16):
        return jax.ShapeDtypeStruct(dims, dtype)

    def over_z(value, d):
        return lax.ppermute(value, "ctx", [(c, c ^ (2 * d)) for c in range(ctx)])

    def over_cores(value):
        return lax.ppermute(value, "ctx", [(c, c ^ 1) for c in range(ctx)])

    def to_user(value, d):
        return lax.ppermute(value, "users", [(u, u ^ d) for u in range(users)])

    def after(value, *others):
        return lax.optimization_barrier((value, *others))[0]

    def over_users(values):
        if OPTS['order'] == 0:
            got = [to_user(values[d], d) for d in range(users - 1, 0, -1)]
            return [values[0]] + got[::-1]
        return [values[0]] + [to_user(values[d], d) for d in range(1, users)]

    kv = hist_kv[0, 0]
    operands = [
        pltpu.VMEM((rows, width), bf16),
        pltpu.VMEM((1, rows), jnp.int32),
        pltpu.VMEM((1, width), jnp.float32),
        pltpu.VMEM((SLICES, width // SLICES, width), bf16),
    ]
    queries = pl.pallas_call(
        functools.partial(query_kernel, cap, users),
        name="query",
        in_specs=[HBM] * 4,
        out_specs=[HBM] * users,
        out_shape=[shape(cap, width)] * users,
        scratch_shapes=operands + [
            pltpu.VMEM((users * cap, width), bf16),
            pltpu.SemaphoreType.DMA((3 + SLICES,)),
            pltpu.SemaphoreType.DMA((users,)),
        ],
        cost_estimate=pl.CostEstimate(flops=OPTS['cq'], bytes_accessed=0, transcendentals=0),
        compiler_params=pltpu.CompilerParams(vmem_limit_bytes=VMEM_MOST),
    )(cand_feat, user_row, gain_in, w_uq[0])
    arrived = over_users(queries)

    env = {'q': queries[0], 'qx': arrived[1], 'qy': arrived[2], 'qd': arrived[3]}

    def gated(value, keys):
        ready = [env[k] for k in keys]
        return after(value, *ready) if ready else value

    held = {0: kv}
    for d in [3, 1] + list(range(4, chips)):
        held[d] = over_z(gated(kv, OPTS['a']) if d == 1 else kv, d)
    env.update(m=held[3], a=held[1])
    gate, pick = call(
        functools.partial(gate_kernel, cap, users), "gate",
        [HBM] * 4,
        [shape(rows, width, dtype=jnp.float32), shape(rows, users * cap)],
        operands + [pltpu.SemaphoreType.DMA((3 + SLICES,))],
        OPTS['cg'],
        gated(cand_feat, ['q'] + OPTS['g']), user_row, gain_in, w_uq[0], vmem=VMEM_MOST,
    )
    env['g'] = gate
    split = call(
        kv_split_kernel, "kv_split", [whole(*kv.shape)],
        [shape(BLK, 2 * wide) for wide in wides], [], OPTS['cs'], held[3],
    )
    env['f'] = split[0]
    last = [over_z(gated(part, OPTS['f' + str(i)]), 1) for i, part in enumerate(split)]
    packed, = call(
        functools.partial(pack_kernel, chips), "pack",
        [SMEM] + [whole(*kv.shape)] * (chips - 1),
        [shape((chips - 1) * BLK, 2 * width)], [], OPTS['cp'],
        hist_mask, gated(kv, OPTS['pk']), *[held[d] for d in early_chips(chips)[1:]],
    )
    packs = [packed, over_cores(gated(packed, OPTS['p']))]
    env['p'] = packs[1]
    returned, first = [], 0
    for chunk, wide in enumerate(wides):
        blocks = [*packs, last[chunk], over_cores(gated(last[chunk], OPTS['s' + str(chunk)]))]
        scored = call(
            functools.partial(attend_kernel, users, chips, first), "attend",
            [SMEM] + [whole(cap, width)] * users + [whole(*block.shape) for block in blocks],
            [shape(cap, wide)] * users,
            [pltpu.VMEM((users * cap, wide), bf16), pltpu.VMEM((chips * BLK, 2 * wide), bf16)],
            OPTS['ca'],
            hist_mask, *arrived, *blocks,
        )
        back = over_users(scored)
        env.update({'s': scored[0], 'rx': back[1], 'ry': back[2], 'rd': back[3]})
        returned += back
        first += wide

    return call(
        functools.partial(finish_kernel, users), "finish",
        [
            whole(rows, width), whole(rows, width), whole(rows, users * cap), whole(1, width),
            whole(width, width),
        ]
        + [whole(*part.shape) for part in returned],
        [shape(rows, width)],
        [pltpu.VMEM((users * cap, width), bf16)],
        OPTS["cf"],
        cand_feat, gate, pick, gain_attn, w_out[0], *returned,
    )[0]


def solution(mesh):
    in_specs = (
        P(("users", "ctx"), None),
        P(("users", "ctx"), None),
        P(None, "users", "ctx", None),
        P("users", None),
        P(),
        P(),
        P(),
        P(),
    )
    out_specs = P(("users", "ctx"), None)
    return jax.shard_map(
        on_device, mesh=mesh, in_specs=in_specs, out_specs=out_specs, check_vma=False
    )
```

```python
import functools

import jax
import jax.numpy as jnp
from jax import lax
from jax.experimental import pallas as pl
from jax.experimental.pallas import tpu as pltpu
from jax.sharding import PartitionSpec as P

BLK = 128
HEAD = 128
OPTS = {'chunks': [4, 4], 'order': 0, 'qs': 0, 'cq': 400000000000, 'cg': 400000000000, 'ca': 1000000000, 'cf': 10000000000, 'm1': [], 'a1': ['f'], 'g': ['a0', 'qx'], 's0': [['qx'], ['g', 'qy'], ['g'], []], 's1': [['s', 'rx'], ['ry'], [], []], 'cp': 0, 'sw': [0, 0], 'p0': [], 'p1': []}
CHUNKS = OPTS['chunks']
SLICES = 2
VMEM_LIMIT = 32 * 1024 * 1024
VMEM_MOST = 60 * 1024 * 1024
HEAVY = 4 * 10**11


def silu_halved(t):
    return t + t * jnp.tanh(t)


def centred_norm(x):
    middle = jnp.mean(x, axis=-1, keepdims=True)
    shifted = x - middle
    spread = jnp.mean(shifted * shifted, axis=-1, keepdims=True)
    return shifted * lax.rsqrt(spread + 1e-05)


def slots_of(user, me, cap, users):
    rows = user.shape[1]
    rel = user ^ me
    places = max(8, users)
    one_hot = rel == lax.broadcasted_iota(jnp.int32, (places, rows), 0)
    one_hot = one_hot.astype(jnp.float32)
    first = lax.broadcasted_iota(jnp.int32, (rows, rows), 0)
    second = lax.broadcasted_iota(jnp.int32, (rows, rows), 1)
    earlier = (first < second).astype(jnp.bfloat16)
    rank = jnp.dot(one_hot.astype(jnp.bfloat16), earlier, preferred_element_type=jnp.float32)
    rank = jnp.sum(rank * one_hot, axis=0, keepdims=True)
    return rel.astype(jnp.float32) * cap + rank


def kv_split_kernel(kv, *outs):
    half = kv.shape[1] // 2
    first = 0
    for out in outs:
        wide = out.shape[1] // 2
        for part in range(2):
            out[:, part * wide:(part + 1) * wide] = kv[
                :, part * half + first:part * half + first + wide
            ]
        first += wide


def load_operands(first_col, feat_in, user_in, gain_in, w_in, feat, user, gain, weights, sems):
    slices, depth, width = weights.shape
    copies = [
        pltpu.make_async_copy(user_in, user, sems.at[0]),
        pltpu.make_async_copy(feat_in, feat, sems.at[1]),
        pltpu.make_async_copy(gain_in, gain, sems.at[2]),
    ]
    for k in range(slices):
        copies.append(
            pltpu.make_async_copy(
                w_in.at[pl.ds(k * depth, depth), pl.ds(first_col, width)],
                weights.at[k],
                sems.at[3 + k],
            )
        )
    for copy in copies:
        copy.start()
    return copies


def project(copies, feat, gain, weights):
    slices, depth, _ = weights.shape
    copies[1].wait()
    copies[2].wait()
    normed = (centred_norm(feat[...].astype(jnp.float32)) * gain[...]).astype(jnp.bfloat16)
    total = None
    for k in range(slices):
        copies[3 + k].wait()
        part = jnp.dot(
            normed[:, k * depth:(k + 1) * depth], weights[k], preferred_element_type=jnp.float32
        )
        total = part if total is None else total + part
    return silu_halved(total * 0.5)


def query_kernel(cap, users, feat_in, user_in, gain_in, w_in, *rest):
    outs, (feat, user, gain, weights, sent, sems, out_sems) = rest[:users], rest[users:]
    rows, width = feat.shape
    copies = load_operands(width, feat_in, user_in, gain_in, w_in, feat, user, gain, weights, sems)
    copies[0].wait()
    slot = slots_of(user[...], lax.axis_index("users"), cap, users)
    places = lax.broadcasted_iota(jnp.int32, (users * cap, rows), 0).astype(jnp.float32)
    pick = (places == slot).astype(jnp.bfloat16)
    query = project(copies, feat, gain, weights).astype(jnp.bfloat16)
    writes = []
    for d in range(users):
        at = slice(d * cap, (d + 1) * cap)
        sent[at, :] = jnp.dot(pick[at, :], query, preferred_element_type=jnp.float32).astype(
            jnp.bfloat16
        )
        writes.append(
            pltpu.make_async_copy(sent.at[pl.ds(d * cap, cap), :], outs[d], out_sems.at[d])
        )
        writes[-1].start()
    for write in writes:
        write.wait()


def gate_kernel(cap, users, feat_in, user_in, gain_in, w_in, gate, pick, feat, user, gain, weights, sems):
    rows, _ = feat.shape
    copies = load_operands(0, feat_in, user_in, gain_in, w_in, feat, user, gain, weights, sems)
    copies[0].wait()
    slot = slots_of(user[...], lax.axis_index("users"), cap, users)
    slot = jnp.transpose(jnp.broadcast_to(slot, (128, rows)))[:, 0:1]
    places = lax.broadcasted_iota(jnp.int32, (rows, users * cap), 1).astype(jnp.float32)
    pick[...] = (places == slot).astype(jnp.bfloat16)
    gate[...] = project(copies, feat, gain, weights)


def pack_kernel(chips, mask, *rest):
    blocks, out = rest[:-1], rest[-1]
    place = lax.axis_index("ctx")
    core, z = place % 2, place // 2
    taken = jnp.int32(0)
    for d, block in enumerate(blocks):
        live = mask[0, 2 * (z ^ d) + core] > 0

        def take(block=block, taken=taken):
            at = pl.multiple_of(taken * BLK, BLK)
            out[pl.ds(at, BLK), :] = block[...]

        pl.when(live)(take)
        taken = taken + live.astype(jnp.int32)


def attend_kernel(users, chips, first, mask, *rest):
    queries, (mine, other) = rest[:users], rest[users:users + 2]
    outs, (all_q, live_kv) = rest[users + 2:2 * users + 2], rest[2 * users + 2:]
    cap, wide = outs[0].shape
    core = lax.axis_index("ctx") % 2
    count = jnp.int32(0)
    for z in range(chips):
        count = count + (mask[0, 2 * z + core] > 0).astype(jnp.int32)
    for slot in range(chips):
        at = slice(slot * BLK, (slot + 1) * BLK)

        def from_mine(at=at):
            live_kv[at, :] = mine[at, :]

        def from_other(at=at, slot=slot):
            source = pl.multiple_of(jnp.maximum(slot - count, 0) * BLK, BLK)
            live_kv[at, :] = other[pl.ds(source, BLK), :]

        pl.when(slot < count)(from_mine)
        pl.when(slot >= count)(from_other)
    for i, q in enumerate(queries):
        all_q[i * cap:(i + 1) * cap, :] = q[:, first:first + wide]
    scale = 0.5 * HEAD ** (-0.5)
    for head in range(wide // HEAD):
        cols = slice(head * HEAD, (head + 1) * HEAD)
        keys = live_kv[:, cols]
        values = live_kv[:, wide + head * HEAD:wide + (head + 1) * HEAD]
        scores = lax.dot_general(
            all_q[:, cols], keys, (((1,), (1,)), ((), ())), preferred_element_type=jnp.float32
        )
        weight = silu_halved(scores * scale).astype(jnp.bfloat16)
        got = jnp.dot(weight, values, preferred_element_type=jnp.float32).astype(jnp.bfloat16)
        for i, out in enumerate(outs):
            out[:, cols] = got[i * cap:(i + 1) * cap, :]


def attend_blocks_kernel(users, chips, first, mask, *rest):
    queries = rest[:users]
    blocks = rest[users:users + 2 * chips]
    outs, (all_q, live_kv) = rest[-2 - users:-2], rest[-2:]
    place = lax.axis_index("ctx")
    core, z = place % 2, place // 2
    cap, wide = outs[0].shape
    taken = jnp.int32(0)
    for d in range(chips):
        for swap in range(2):
            live = mask[0, 2 * (z ^ d) + (core ^ swap)] > 0

            def take(block=blocks[2 * d + swap], taken=taken):
                at = pl.multiple_of(taken * BLK, BLK)
                live_kv[pl.ds(at, BLK), :] = block[...]

            pl.when(live)(take)
            taken = jnp.minimum(taken + live.astype(jnp.int32), chips - 1)
    for i, q in enumerate(queries):
        all_q[i * cap:(i + 1) * cap, :] = q[:, first:first + wide]
    scale = 0.5 * HEAD ** (-0.5)
    for head in range(wide // HEAD):
        cols = slice(head * HEAD, (head + 1) * HEAD)
        keys = live_kv[:, cols]
        values = live_kv[:, wide + head * HEAD:wide + (head + 1) * HEAD]
        scores = lax.dot_general(
            all_q[:, cols], keys, (((1,), (1,)), ((), ())), preferred_element_type=jnp.float32
        )
        weight = silu_halved(scores * scale).astype(jnp.bfloat16)
        got = jnp.dot(weight, values, preferred_element_type=jnp.float32).astype(jnp.bfloat16)
        for i, out in enumerate(outs):
            out[:, cols] = got[i * cap:(i + 1) * cap, :]


def finish_kernel(users, feat, gate, pick, gain, w_out, *rest):
    parts, out, back = rest[:-2], rest[-2], rest[-1]
    first = 0
    for chunk in range(len(parts) // users):
        cap, wide = parts[chunk * users].shape
        for d in range(users):
            part = parts[chunk * users + d]
            back[d * cap:(d + 1) * cap, first:first + wide] = part[...]
        first += wide
    attended = jnp.dot(pick[...], back[...], preferred_element_type=jnp.float32)
    mixed = (centred_norm(attended) * gain[...] * gate[...]).astype(jnp.bfloat16)
    grown = jnp.dot(mixed, w_out[...], preferred_element_type=jnp.float32)
    out[...] = (feat[...].astype(jnp.float32) + grown).astype(jnp.bfloat16)


SMEM = pl.BlockSpec(memory_space=pltpu.SMEM)
HBM = pl.BlockSpec(memory_space=pltpu.HBM)


def whole(*dims, at=None):
    return pl.BlockSpec(dims, lambda i: at or (0,) * len(dims))


def call(kernel, name, in_specs, out_shape, scratch, flops, *args, vmem=VMEM_LIMIT):
    moved = sum(a.size * a.dtype.itemsize for a in args)
    return pl.pallas_call(
        kernel,
        name=name,
        grid=(1,),
        in_specs=in_specs,
        out_specs=[whole(*s.shape) for s in out_shape],
        out_shape=out_shape,
        scratch_shapes=scratch,
        cost_estimate=pl.CostEstimate(flops=flops, bytes_accessed=moved if flops else 0, transcendentals=0),
        compiler_params=pltpu.CompilerParams(vmem_limit_bytes=vmem),
    )(*args)


def on_device(cand_feat, cand_user, hist_kv, hist_mask, gain_in, w_uq, gain_attn, w_out):
    users = lax.axis_size("users")
    ctx = lax.axis_size("ctx")
    chips = ctx // 2
    rows, width = cand_feat.shape
    cap = 2 * rows // users
    wides = [heads * HEAD for heads in CHUNKS]
    bf16 = jnp.bfloat16
    user_row = cand_user.reshape(1, rows)

    def shape(*dims, dtype=bf16):
        return jax.ShapeDtypeStruct(dims, dtype)

    def over_z(value, d):
        return lax.ppermute(value, "ctx", [(c, c ^ (2 * d)) for c in range(ctx)])

    def over_cores(value):
        return lax.ppermute(value, "ctx", [(c, c ^ 1) for c in range(ctx)])

    def to_user(value, d):
        return lax.ppermute(value, "users", [(u, u ^ d) for u in range(users)])

    def after(value, *others):
        return lax.optimization_barrier((value, *others))[0]

    def over_users(values):
        if OPTS['order'] == 0:
            got = [to_user(values[d], d) for d in range(users - 1, 0, -1)]
            return [values[0]] + got[::-1]
        return [values[0]] + [to_user(values[d], d) for d in range(1, users)]

    kv = hist_kv[0, 0]
    split = call(
        kv_split_kernel, "kv_split", [whole(*kv.shape)],
        [shape(BLK, 2 * wide) for wide in wides], [], 0, kv,
    )

    operands = [
        pltpu.VMEM((rows, width), bf16),
        pltpu.VMEM((1, rows), jnp.int32),
        pltpu.VMEM((1, width), jnp.float32),
        pltpu.VMEM((SLICES, width // SLICES, width), bf16),
    ]
    queries = pl.pallas_call(
        functools.partial(query_kernel, cap, users),
        name="query",
        in_specs=[HBM] * 4,
        out_specs=[HBM] * users,
        out_shape=[shape(cap, width)] * users,
        scratch_shapes=operands + [
            pltpu.VMEM((users * cap, width), bf16),
            pltpu.SemaphoreType.DMA((3 + SLICES,)),
            pltpu.SemaphoreType.DMA((users,)),
        ],
        cost_estimate=pl.CostEstimate(flops=OPTS['cq'], bytes_accessed=0, transcendentals=0),
        compiler_params=pltpu.CompilerParams(vmem_limit_bytes=VMEM_MOST),
    )(*([after(cand_feat, split[0])] if OPTS['qs'] else [cand_feat]), user_row, gain_in, w_uq[0])
    arrived = over_users(queries)

    returned, first, env = [], 0, {}
    env.update({'qx': arrived[1], 'qy': arrived[2], 'qd': arrived[3], 'q': queries[0]})

    def gated(value, keys):
        ready = [env[k] for k in keys]
        return after(value, *ready) if ready else value

    for chunk, wide in enumerate(wides):
        held = {0: split[chunk]}
        far = near = split[chunk]
        if chunk:
            c = str(chunk - 1)
            far = gated(far, [k + c if k in 'maf' else k for k in OPTS['m1']])
            near = gated(near, [k + c if k in 'maf' else k for k in OPTS['a1']])
        for d in [3, 1, 2] + list(range(4, chips)):
            held[d] = over_z(held[3], 1) if d == 2 else over_z(near if d == 1 else far, d)
        env.update({'a' + str(chunk): held[1], 'm' + str(chunk): held[3], 'f' + str(chunk): held[2]})
        if chunk == 0:
            gate, pick = call(
                functools.partial(gate_kernel, cap, users), "gate",
                [HBM] * 4,
                [shape(rows, width, dtype=jnp.float32), shape(rows, users * cap)],
                operands + [pltpu.SemaphoreType.DMA((3 + SLICES,))],
                OPTS['cg'],
                gated(cand_feat, ['q'] + OPTS['g']), user_row, gain_in, w_uq[0], vmem=VMEM_MOST,
            )
            env['g'] = gate
        if OPTS['sw'][chunk]:
            keys = OPTS['p0'] if chunk == 0 else OPTS['p1']
            packed, = call(
                functools.partial(pack_kernel, chips), "pack",
                [SMEM] + [whole(BLK, 2 * wide)] * chips,
                [shape(chips * BLK, 2 * wide)], [], OPTS['cp'],
                hist_mask, gated(held[0], keys), *[held[d] for d in range(1, chips)],
            )
            blocks, kernel = [packed, over_cores(packed)], attend_kernel
        else:
            blocks, kernel = [], attend_blocks_kernel
            for d in range(chips):
                keys = OPTS['s0' if chunk == 0 else 's1'][d % 4]
                blocks += [held[d], over_cores(gated(held[d], keys))]
        scored = call(
            functools.partial(kernel, users, chips, first), "attend",
            [SMEM] + [whole(cap, width)] * users + [whole(*block.shape) for block in blocks],
            [shape(cap, wide)] * users,
            [pltpu.VMEM((users * cap, wide), bf16), pltpu.VMEM((chips * BLK, 2 * wide), bf16)],
            OPTS['ca'],
            hist_mask, *arrived, *blocks,
        )
        back = over_users(scored)
        env.update({'s': scored[0], 'rx': back[1], 'ry': back[2], 'rd': back[3]})
        returned += back
        first += wide

    return call(
        functools.partial(finish_kernel, users), "finish",
        [
            whole(rows, width), whole(rows, width), whole(rows, users * cap), whole(1, width),
            whole(width, width),
        ]
        + [whole(*part.shape) for part in returned],
        [shape(rows, width)],
        [pltpu.VMEM((users * cap, width), bf16)],
        OPTS["cf"],
        cand_feat, gate, pick, gain_attn, w_out[0], *returned,
    )[0]


def solution(mesh):
    in_specs = (
        P(("users", "ctx"), None),
        P(("users", "ctx"), None),
        P(None, "users", "ctx", None),
        P("users", None),
        P(),
        P(),
        P(),
        P(),
    )
    out_specs = P(("users", "ctx"), None)
    return jax.shard_map(
        on_device, mesh=mesh, in_specs=in_specs, out_specs=out_specs, check_vma=False
    )
```

```python
import functools

import jax
import jax.numpy as jnp
from jax import lax
from jax.experimental import pallas as pl
from jax.experimental.pallas import tpu as pltpu
from jax.sharding import PartitionSpec as P

BLK = 128
HEAD = 128
OPTS = {'chunks': (4, 4), 'order': 0, 'qs': 1, 'cq': 400000000000, 'cg': 400000000000, 'ca': 2000000000, 'cf': 1000000000, 'cp': 0, 'sw': (0, 0), 'p0': [], 'p1': [], 'm1': ['m', 'g'], 'a1': ['a', 'g'], 'g': [], 's0': [['qx'], ['qx'], [], ['qx']], 's1': [[], ['s'], ['rd'], []]}
CHUNKS = OPTS['chunks']
SLICES = 2
VMEM_LIMIT = 32 * 1024 * 1024
VMEM_MOST = 60 * 1024 * 1024
HEAVY = 4 * 10**11


def silu_halved(t):
    return t + t * jnp.tanh(t)


def centred_norm(x):
    middle = jnp.mean(x, axis=-1, keepdims=True)
    shifted = x - middle
    spread = jnp.mean(shifted * shifted, axis=-1, keepdims=True)
    return shifted * lax.rsqrt(spread + 1e-05)


def slots_of(user, me, cap, users):
    rows = user.shape[1]
    rel = user ^ me
    places = max(8, users)
    one_hot = rel == lax.broadcasted_iota(jnp.int32, (places, rows), 0)
    one_hot = one_hot.astype(jnp.float32)
    first = lax.broadcasted_iota(jnp.int32, (rows, rows), 0)
    second = lax.broadcasted_iota(jnp.int32, (rows, rows), 1)
    earlier = (first < second).astype(jnp.bfloat16)
    rank = jnp.dot(one_hot.astype(jnp.bfloat16), earlier, preferred_element_type=jnp.float32)
    rank = jnp.sum(rank * one_hot, axis=0, keepdims=True)
    return rel.astype(jnp.float32) * cap + rank


def kv_split_kernel(kv, *outs):
    half = kv.shape[1] // 2
    first = 0
    for out in outs:
        wide = out.shape[1] // 2
        for part in range(2):
            out[:, part * wide:(part + 1) * wide] = kv[
                :, part * half + first:part * half + first + wide
            ]
        first += wide


def load_operands(first_col, feat_in, user_in, gain_in, w_in, feat, user, gain, weights, sems):
    slices, depth, width = weights.shape
    copies = [
        pltpu.make_async_copy(user_in, user, sems.at[0]),
        pltpu.make_async_copy(feat_in, feat, sems.at[1]),
        pltpu.make_async_copy(gain_in, gain, sems.at[2]),
    ]
    for k in range(slices):
        copies.append(
            pltpu.make_async_copy(
                w_in.at[pl.ds(k * depth, depth), pl.ds(first_col, width)],
                weights.at[k],
                sems.at[3 + k],
            )
        )
    for copy in copies:
        copy.start()
    return copies


def project(copies, feat, gain, weights):
    slices, depth, _ = weights.shape
    copies[1].wait()
    copies[2].wait()
    normed = (centred_norm(feat[...].astype(jnp.float32)) * gain[...]).astype(jnp.bfloat16)
    total = None
    for k in range(slices):
        copies[3 + k].wait()
        part = jnp.dot(
            normed[:, k * depth:(k + 1) * depth], weights[k], preferred_element_type=jnp.float32
        )
        total = part if total is None else total + part
    return silu_halved(total * 0.5)


def query_kernel(cap, users, feat_in, user_in, gain_in, w_in, *rest):
    outs, (feat, user, gain, weights, sent, sems, out_sems) = rest[:users], rest[users:]
    rows, width = feat.shape
    copies = load_operands(width, feat_in, user_in, gain_in, w_in, feat, user, gain, weights, sems)
    copies[0].wait()
    slot = slots_of(user[...], lax.axis_index("users"), cap, users)
    places = lax.broadcasted_iota(jnp.int32, (users * cap, rows), 0).astype(jnp.float32)
    pick = (places == slot).astype(jnp.bfloat16)
    query = project(copies, feat, gain, weights).astype(jnp.bfloat16)
    writes = []
    for d in range(users):
        at = slice(d * cap, (d + 1) * cap)
        sent[at, :] = jnp.dot(pick[at, :], query, preferred_element_type=jnp.float32).astype(
            jnp.bfloat16
        )
        writes.append(
            pltpu.make_async_copy(sent.at[pl.ds(d * cap, cap), :], outs[d], out_sems.at[d])
        )
        writes[-1].start()
    for write in writes:
        write.wait()


def gate_kernel(cap, users, feat_in, user_in, gain_in, w_in, gate, pick, feat, user, gain, weights, sems):
    rows, _ = feat.shape
    copies = load_operands(0, feat_in, user_in, gain_in, w_in, feat, user, gain, weights, sems)
    copies[0].wait()
    slot = slots_of(user[...], lax.axis_index("users"), cap, users)
    slot = jnp.transpose(jnp.broadcast_to(slot, (128, rows)))[:, 0:1]
    places = lax.broadcasted_iota(jnp.int32, (rows, users * cap), 1).astype(jnp.float32)
    pick[...] = (places == slot).astype(jnp.bfloat16)
    gate[...] = project(copies, feat, gain, weights)


def pack_kernel(chips, mask, *rest):
    blocks, out = rest[:-1], rest[-1]
    place = lax.axis_index("ctx")
    core, z = place % 2, place // 2
    taken = jnp.int32(0)
    for d, block in enumerate(blocks):
        live = mask[0, 2 * (z ^ d) + core] > 0

        def take(block=block, taken=taken):
            at = pl.multiple_of(taken * BLK, BLK)
            out[pl.ds(at, BLK), :] = block[...]

        pl.when(live)(take)
        taken = taken + live.astype(jnp.int32)


def attend_kernel(users, chips, mask, *rest):
    queries, (mine, other) = rest[:users], rest[users:users + 2]
    outs, (all_q, live_kv) = rest[users + 2:2 * users + 2], rest[2 * users + 2:]
    cap, wide = outs[0].shape
    core = lax.axis_index("ctx") % 2
    count = jnp.int32(0)
    for z in range(chips):
        count = count + (mask[0, 2 * z + core] > 0).astype(jnp.int32)
    for slot in range(chips):
        at = slice(slot * BLK, (slot + 1) * BLK)

        def from_mine(at=at):
            live_kv[at, :] = mine[at, :]

        def from_other(at=at, slot=slot):
            source = pl.multiple_of(jnp.maximum(slot - count, 0) * BLK, BLK)
            live_kv[at, :] = other[pl.ds(source, BLK), :]

        pl.when(slot < count)(from_mine)
        pl.when(slot >= count)(from_other)
    for i, q in enumerate(queries):
        all_q[i * cap:(i + 1) * cap, :] = q[...]
    scale = 0.5 * HEAD ** (-0.5)
    for head in range(wide // HEAD):
        cols = slice(head * HEAD, (head + 1) * HEAD)
        keys = live_kv[:, cols]
        values = live_kv[:, wide + head * HEAD:wide + (head + 1) * HEAD]
        scores = lax.dot_general(
            all_q[:, cols], keys, (((1,), (1,)), ((), ())), preferred_element_type=jnp.float32
        )
        weight = silu_halved(scores * scale).astype(jnp.bfloat16)
        got = jnp.dot(weight, values, preferred_element_type=jnp.float32).astype(jnp.bfloat16)
        for i, out in enumerate(outs):
            out[:, cols] = got[i * cap:(i + 1) * cap, :]


def attend_blocks_kernel(users, chips, mask, *rest):
    queries = rest[:users]
    blocks = rest[users:users + 2 * chips]
    outs, (all_q, live_kv) = rest[-2 - users:-2], rest[-2:]
    place = lax.axis_index("ctx")
    core, z = place % 2, place // 2
    cap, wide = outs[0].shape
    taken = jnp.int32(0)
    for d in range(chips):
        for swap in range(2):
            live = mask[0, 2 * (z ^ d) + (core ^ swap)] > 0

            def take(block=blocks[2 * d + swap], taken=taken):
                at = pl.multiple_of(taken * BLK, BLK)
                live_kv[pl.ds(at, BLK), :] = block[...]

            pl.when(live)(take)
            taken = jnp.minimum(taken + live.astype(jnp.int32), chips - 1)
    for i, q in enumerate(queries):
        all_q[i * cap:(i + 1) * cap, :] = q[...]
    scale = 0.5 * HEAD ** (-0.5)
    for head in range(wide // HEAD):
        cols = slice(head * HEAD, (head + 1) * HEAD)
        keys = live_kv[:, cols]
        values = live_kv[:, wide + head * HEAD:wide + (head + 1) * HEAD]
        scores = lax.dot_general(
            all_q[:, cols], keys, (((1,), (1,)), ((), ())), preferred_element_type=jnp.float32
        )
        weight = silu_halved(scores * scale).astype(jnp.bfloat16)
        got = jnp.dot(weight, values, preferred_element_type=jnp.float32).astype(jnp.bfloat16)
        for i, out in enumerate(outs):
            out[:, cols] = got[i * cap:(i + 1) * cap, :]


def finish_kernel(users, feat, gate, pick, gain, w_out, *rest):
    parts, out, back = rest[:-2], rest[-2], rest[-1]
    first = 0
    for chunk in range(len(parts) // users):
        cap, wide = parts[chunk * users].shape
        for d in range(users):
            part = parts[chunk * users + d]
            back[d * cap:(d + 1) * cap, first:first + wide] = part[...]
        first += wide
    attended = jnp.dot(pick[...], back[...], preferred_element_type=jnp.float32)
    mixed = (centred_norm(attended) * gain[...] * gate[...]).astype(jnp.bfloat16)
    grown = jnp.dot(mixed, w_out[...], preferred_element_type=jnp.float32)
    out[...] = (feat[...].astype(jnp.float32) + grown).astype(jnp.bfloat16)


SMEM = pl.BlockSpec(memory_space=pltpu.SMEM)
HBM = pl.BlockSpec(memory_space=pltpu.HBM)


def whole(*dims, at=None):
    return pl.BlockSpec(dims, lambda i: at or (0,) * len(dims))


def call(kernel, name, in_specs, out_shape, scratch, flops, *args, vmem=VMEM_LIMIT):
    moved = sum(a.size * a.dtype.itemsize for a in args)
    return pl.pallas_call(
        kernel,
        name=name,
        grid=(1,),
        in_specs=in_specs,
        out_specs=[whole(*s.shape) for s in out_shape],
        out_shape=out_shape,
        scratch_shapes=scratch,
        cost_estimate=pl.CostEstimate(flops=flops, bytes_accessed=moved if flops else 0, transcendentals=0),
        compiler_params=pltpu.CompilerParams(vmem_limit_bytes=vmem),
    )(*args)


def on_device(cand_feat, cand_user, hist_kv, hist_mask, gain_in, w_uq, gain_attn, w_out):
    users = lax.axis_size("users")
    ctx = lax.axis_size("ctx")
    chips = ctx // 2
    rows, width = cand_feat.shape
    cap = 2 * rows // users
    wides = [heads * HEAD for heads in CHUNKS]
    bf16 = jnp.bfloat16
    user_row = cand_user.reshape(1, rows)

    def shape(*dims, dtype=bf16):
        return jax.ShapeDtypeStruct(dims, dtype)

    def over_z(value, d):
        return lax.ppermute(value, "ctx", [(c, c ^ (2 * d)) for c in range(ctx)])

    def over_cores(value):
        return lax.ppermute(value, "ctx", [(c, c ^ 1) for c in range(ctx)])

    def to_user(value, d):
        return lax.ppermute(value, "users", [(u, u ^ d) for u in range(users)])

    def after(value, *others):
        return lax.optimization_barrier((value, *others))[0]

    def over_users(values):
        if OPTS['order'] == 0:
            got = [to_user(values[d], d) for d in range(users - 1, 0, -1)]
            return [values[0]] + got[::-1]
        return [values[0]] + [to_user(values[d], d) for d in range(1, users)]

    kv = hist_kv[0, 0]
    split = call(
        kv_split_kernel, "kv_split", [whole(*kv.shape)],
        [shape(BLK, 2 * wide) for wide in wides], [], 0, kv,
    )

    operands = [
        pltpu.VMEM((rows, width), bf16),
        pltpu.VMEM((1, rows), jnp.int32),
        pltpu.VMEM((1, width), jnp.float32),
        pltpu.VMEM((SLICES, width // SLICES, width), bf16),
    ]
    queries = pl.pallas_call(
        functools.partial(query_kernel, cap, users),
        name="query",
        in_specs=[HBM] * 4,
        out_specs=[HBM] * users,
        out_shape=[shape(cap, width)] * users,
        scratch_shapes=operands + [
            pltpu.VMEM((users * cap, width), bf16),
            pltpu.SemaphoreType.DMA((3 + SLICES,)),
            pltpu.SemaphoreType.DMA((users,)),
        ],
        cost_estimate=pl.CostEstimate(flops=OPTS['cq'], bytes_accessed=0, transcendentals=0),
        compiler_params=pltpu.CompilerParams(vmem_limit_bytes=VMEM_MOST),
    )(*([after(cand_feat, split[0])] if OPTS['qs'] else [cand_feat]), user_row, gain_in, w_uq[0])
    arrived = over_users(queries)

    returned, first, env = [], 0, {}
    env.update({'qx': arrived[1], 'qy': arrived[2], 'qd': arrived[3], 'q': queries[0]})

    def gated(value, keys):
        ready = [env[k] for k in keys]
        return after(value, *ready) if ready else value

    for chunk, wide in enumerate(wides):
        held = {0: split[chunk]}
        far = near = split[chunk]
        if chunk:
            c = str(chunk - 1)
            far = gated(far, [k + c if k in 'maf' else k for k in OPTS['m1']])
            near = gated(near, [k + c if k in 'maf' else k for k in OPTS['a1']])
        for d in [3, 1, 2] + list(range(4, chips)):
            held[d] = over_z(held[3], 1) if d == 2 else over_z(near if d == 1 else far, d)
        env.update({'a' + str(chunk): held[1], 'm' + str(chunk): held[3], 'f' + str(chunk): held[2]})
        if chunk == 0:
            gate, pick = call(
                functools.partial(gate_kernel, cap, users), "gate",
                [HBM] * 4,
                [shape(rows, width, dtype=jnp.float32), shape(rows, users * cap)],
                operands + [pltpu.SemaphoreType.DMA((3 + SLICES,))],
                OPTS['cg'],
                gated(cand_feat, ['q'] + OPTS['g']), user_row, gain_in, w_uq[0], vmem=VMEM_MOST,
            )
            env['g'] = gate
        if OPTS['sw'][chunk]:
            keys = OPTS['p0'] if chunk == 0 else OPTS['p1']
            packed, = call(
                functools.partial(pack_kernel, chips), "pack",
                [SMEM] + [whole(BLK, 2 * wide)] * chips,
                [shape(chips * BLK, 2 * wide)], [], OPTS['cp'],
                hist_mask, gated(held[0], keys), *[held[d] for d in range(1, chips)],
            )
            blocks, kernel = [packed, over_cores(packed)], attend_kernel
        else:
            blocks, kernel = [], attend_blocks_kernel
            for d in range(chips):
                keys = OPTS['s0' if chunk == 0 else 's1'][d % 4]
                blocks += [held[d], over_cores(gated(held[d], keys))]
        scored = call(
            functools.partial(kernel, users, chips), "attend",
            [SMEM] + [whole(cap, wide, at=(0, chunk))] * users + [whole(*block.shape) for block in blocks],
            [shape(cap, wide)] * users,
            [pltpu.VMEM((users * cap, wide), bf16), pltpu.VMEM((chips * BLK, 2 * wide), bf16)],
            OPTS['ca'],
            hist_mask, *arrived, *blocks,
        )
        back = over_users(scored)
        env.update({'s': scored[0], 'rx': back[1], 'ry': back[2], 'rd': back[3]})
        returned += back
        first += wide

    return call(
        functools.partial(finish_kernel, users), "finish",
        [
            whole(rows, width), whole(rows, width), whole(rows, users * cap), whole(1, width),
            whole(width, width),
        ]
        + [whole(*part.shape) for part in returned],
        [shape(rows, width)],
        [pltpu.VMEM((users * cap, width), bf16)],
        OPTS["cf"],
        cand_feat, gate, pick, gain_attn, w_out[0], *returned,
    )[0]


def solution(mesh):
    in_specs = (
        P(("users", "ctx"), None),
        P(("users", "ctx"), None),
        P(None, "users", "ctx", None),
        P("users", None),
        P(),
        P(),
        P(),
        P(),
    )
    out_specs = P(("users", "ctx"), None)
    return jax.shard_map(
        on_device, mesh=mesh, in_specs=in_specs, out_specs=out_specs, check_vma=False
    )
```

```python
import functools

import jax
import jax.numpy as jnp
from jax import lax
from jax.experimental import pallas as pl
from jax.experimental.pallas import tpu as pltpu
from jax.sharding import PartitionSpec as P

BLK = 128
HEAD = 128
OPTS = {'chunks': [4, 4], 'order': 0, 'qs': 1, 'cq': 0, 'cg': 400000000000, 'ca': 2000000000, 'cf': 400000000000, 'cp': 0, 'sw': [0, 0], 'p0': [], 'p1': [], 'm1': ['m', 'a'], 'a1': ['f', 'g'], 'g': [], 's0': [['qx'], [], ['g'], ['g', 'qx']], 's1': [[], ['s'], ['rd'], []]}
CHUNKS = OPTS['chunks']
SLICES = 2
VMEM_LIMIT = 32 * 1024 * 1024
VMEM_MOST = 60 * 1024 * 1024
HEAVY = 4 * 10**11


def silu_halved(t):
    return t + t * jnp.tanh(t)


def centred_norm(x):
    middle = jnp.mean(x, axis=-1, keepdims=True)
    shifted = x - middle
    spread = jnp.mean(shifted * shifted, axis=-1, keepdims=True)
    return shifted * lax.rsqrt(spread + 1e-05)


def slots_of(user, me, cap, users):
    rows = user.shape[1]
    rel = user ^ me
    places = max(8, users)
    one_hot = rel == lax.broadcasted_iota(jnp.int32, (places, rows), 0)
    one_hot = one_hot.astype(jnp.float32)
    first = lax.broadcasted_iota(jnp.int32, (rows, rows), 0)
    second = lax.broadcasted_iota(jnp.int32, (rows, rows), 1)
    earlier = (first < second).astype(jnp.bfloat16)
    rank = jnp.dot(one_hot.astype(jnp.bfloat16), earlier, preferred_element_type=jnp.float32)
    rank = jnp.sum(rank * one_hot, axis=0, keepdims=True)
    return rel.astype(jnp.float32) * cap + rank


def kv_split_kernel(kv, *outs):
    half = kv.shape[1] // 2
    first = 0
    for out in outs:
        wide = out.shape[1] // 2
        for part in range(2):
            out[:, part * wide:(part + 1) * wide] = kv[
                :, part * half + first:part * half + first + wide
            ]
        first += wide


def load_operands(first_col, feat_in, user_in, gain_in, w_in, feat, user, gain, weights, sems):
    slices, depth, width = weights.shape
    copies = [
        pltpu.make_async_copy(user_in, user, sems.at[0]),
        pltpu.make_async_copy(feat_in, feat, sems.at[1]),
        pltpu.make_async_copy(gain_in, gain, sems.at[2]),
    ]
    for k in range(slices):
        copies.append(
            pltpu.make_async_copy(
                w_in.at[pl.ds(k * depth, depth), pl.ds(first_col, width)],
                weights.at[k],
                sems.at[3 + k],
            )
        )
    for copy in copies:
        copy.start()
    return copies


def project(copies, feat, gain, weights):
    slices, depth, _ = weights.shape
    copies[1].wait()
    copies[2].wait()
    normed = (centred_norm(feat[...].astype(jnp.float32)) * gain[...]).astype(jnp.bfloat16)
    total = None
    for k in range(slices):
        copies[3 + k].wait()
        part = jnp.dot(
            normed[:, k * depth:(k + 1) * depth], weights[k], preferred_element_type=jnp.float32
        )
        total = part if total is None else total + part
    return silu_halved(total * 0.5)


def query_kernel(cap, users, feat_in, user_in, gain_in, w_in, *rest):
    outs, (feat, user, gain, weights, sent, sems, out_sems) = rest[:users], rest[users:]
    rows, width = feat.shape
    copies = load_operands(width, feat_in, user_in, gain_in, w_in, feat, user, gain, weights, sems)
    copies[0].wait()
    slot = slots_of(user[...], lax.axis_index("users"), cap, users)
    places = lax.broadcasted_iota(jnp.int32, (users * cap, rows), 0).astype(jnp.float32)
    pick = (places == slot).astype(jnp.bfloat16)
    query = project(copies, feat, gain, weights).astype(jnp.bfloat16)
    writes = []
    for d in range(users):
        at = slice(d * cap, (d + 1) * cap)
        sent[at, :] = jnp.dot(pick[at, :], query, preferred_element_type=jnp.float32).astype(
            jnp.bfloat16
        )
        writes.append(
            pltpu.make_async_copy(sent.at[pl.ds(d * cap, cap), :], outs[d], out_sems.at[d])
        )
        writes[-1].start()
    for write in writes:
        write.wait()


def gate_kernel(cap, users, feat_in, user_in, gain_in, w_in, gate, pick, feat, user, gain, weights, sems):
    rows, _ = feat.shape
    copies = load_operands(0, feat_in, user_in, gain_in, w_in, feat, user, gain, weights, sems)
    copies[0].wait()
    slot = slots_of(user[...], lax.axis_index("users"), cap, users)
    slot = jnp.transpose(jnp.broadcast_to(slot, (128, rows)))[:, 0:1]
    places = lax.broadcasted_iota(jnp.int32, (rows, users * cap), 1).astype(jnp.float32)
    pick[...] = (places == slot).astype(jnp.bfloat16)
    gate[...] = project(copies, feat, gain, weights)


def attend_kernel(users, chips, first, mask, *rest):
    queries = rest[:users]
    blocks = rest[users:users + 2 * chips]
    outs, (all_q, live_kv, q_sems, kv_sems) = rest[-4 - users:-4], rest[-4:]
    cap, wide = outs[0].shape
    place = lax.axis_index("ctx")
    core, z = place % 2, place // 2
    fetched, taken = [], jnp.int32(0)
    for d in range(chips):
        for swap in range(2):
            live = mask[0, 2 * (z ^ d) + (core ^ swap)] > 0
            at = pl.multiple_of(taken * BLK, BLK)
            copy = pltpu.make_async_copy(
                blocks[2 * d + swap], live_kv.at[pl.ds(at, BLK), :], kv_sems.at[2 * d + swap]
            )
            pl.when(live)(copy.start)
            fetched.append((live, copy))
            taken = jnp.minimum(taken + live.astype(jnp.int32), chips - 1)
    loads = []
    for i, q in enumerate(queries):
        loads.append(
            pltpu.make_async_copy(
                q.at[:, pl.ds(first, wide)], all_q.at[pl.ds(i * cap, cap), :], q_sems.at[i]
            )
        )
        loads[-1].start()
    for live, copy in fetched:
        pl.when(live)(copy.wait)
    for load in loads:
        load.wait()
    scale = 0.5 * HEAD ** (-0.5)
    for head in range(wide // HEAD):
        cols = slice(head * HEAD, (head + 1) * HEAD)
        keys = live_kv[:, cols]
        values = live_kv[:, wide + head * HEAD:wide + (head + 1) * HEAD]
        scores = lax.dot_general(
            all_q[:, cols], keys, (((1,), (1,)), ((), ())), preferred_element_type=jnp.float32
        )
        weight = silu_halved(scores * scale).astype(jnp.bfloat16)
        got = jnp.dot(weight, values, preferred_element_type=jnp.float32).astype(jnp.bfloat16)
        for i, out in enumerate(outs):
            out[:, cols] = got[i * cap:(i + 1) * cap, :]


def finish_kernel(users, feat_in, gate_in, pick_in, gain_in, w_in, *rest):
    parts, out = rest[:-8], rest[-8]
    back, pick, gate, gain, weights, feat, sems = rest[-7:]
    loads, first = [], 0
    for chunk in range(len(parts) // users):
        cap, wide = parts[chunk * users].shape
        for d in range(users):
            loads.append(
                pltpu.make_async_copy(
                    parts[chunk * users + d],
                    back.at[pl.ds(d * cap, cap), pl.ds(first, wide)],
                    sems.at[5 + chunk * users + d],
                )
            )
        first += wide
    loads.append(pltpu.make_async_copy(pick_in, pick, sems.at[0]))
    gains = [
        pltpu.make_async_copy(gate_in, gate, sems.at[1]),
        pltpu.make_async_copy(gain_in, gain, sems.at[2]),
    ]
    ends = [
        pltpu.make_async_copy(w_in, weights, sems.at[3]),
        pltpu.make_async_copy(feat_in, feat, sems.at[4]),
    ]
    for copy in loads + gains + ends:
        copy.start()
    for copy in loads:
        copy.wait()
    attended = jnp.dot(pick[...], back[...], preferred_element_type=jnp.float32)
    normed = centred_norm(attended)
    for copy in gains:
        copy.wait()
    mixed = (normed * gain[...] * gate[...]).astype(jnp.bfloat16)
    for copy in ends:
        copy.wait()
    grown = jnp.dot(mixed, weights[...], preferred_element_type=jnp.float32)
    out[...] = (feat[...].astype(jnp.float32) + grown).astype(jnp.bfloat16)


SMEM = pl.BlockSpec(memory_space=pltpu.SMEM)
HBM = pl.BlockSpec(memory_space=pltpu.HBM)
ANY = pl.BlockSpec(memory_space=pl.ANY)


def whole(*dims, at=None):
    return pl.BlockSpec(dims, lambda i: at or (0,) * len(dims))


def call(kernel, name, in_specs, out_shape, scratch, flops, *args, vmem=VMEM_LIMIT):
    moved = sum(a.size * a.dtype.itemsize for a in args)
    return pl.pallas_call(
        kernel,
        name=name,
        grid=(1,),
        in_specs=in_specs,
        out_specs=[whole(*s.shape) for s in out_shape],
        out_shape=out_shape,
        scratch_shapes=scratch,
        cost_estimate=pl.CostEstimate(flops=flops, bytes_accessed=moved if flops else 0, transcendentals=0),
        compiler_params=pltpu.CompilerParams(vmem_limit_bytes=vmem),
    )(*args)


def on_device(cand_feat, cand_user, hist_kv, hist_mask, gain_in, w_uq, gain_attn, w_out):
    users = lax.axis_size("users")
    ctx = lax.axis_size("ctx")
    chips = ctx // 2
    rows, width = cand_feat.shape
    cap = 2 * rows // users
    wides = [heads * HEAD for heads in CHUNKS]
    bf16 = jnp.bfloat16
    user_row = cand_user.reshape(1, rows)

    def shape(*dims, dtype=bf16):
        return jax.ShapeDtypeStruct(dims, dtype)

    def over_z(value, d):
        return lax.ppermute(value, "ctx", [(c, c ^ (2 * d)) for c in range(ctx)])

    def over_cores(value):
        return lax.ppermute(value, "ctx", [(c, c ^ 1) for c in range(ctx)])

    def to_user(value, d):
        return lax.ppermute(value, "users", [(u, u ^ d) for u in range(users)])

    def after(value, *others):
        return lax.optimization_barrier((value, *others))[0]

    def over_users(values):
        if OPTS['order'] == 0:
            got = [to_user(values[d], d) for d in range(users - 1, 0, -1)]
            return [values[0]] + got[::-1]
        return [values[0]] + [to_user(values[d], d) for d in range(1, users)]

    kv = hist_kv[0, 0]
    split = call(
        kv_split_kernel, "kv_split", [whole(*kv.shape)],
        [shape(BLK, 2 * wide) for wide in wides], [], 0, kv,
    )

    operands = [
        pltpu.VMEM((rows, width), bf16),
        pltpu.VMEM((1, rows), jnp.int32),
        pltpu.VMEM((1, width), jnp.float32),
        pltpu.VMEM((SLICES, width // SLICES, width), bf16),
    ]
    queries = pl.pallas_call(
        functools.partial(query_kernel, cap, users),
        name="query",
        in_specs=[HBM] * 4,
        out_specs=[HBM] * users,
        out_shape=[shape(cap, width)] * users,
        scratch_shapes=operands + [
            pltpu.VMEM((users * cap, width), bf16),
            pltpu.SemaphoreType.DMA((3 + SLICES,)),
            pltpu.SemaphoreType.DMA((users,)),
        ],
        cost_estimate=pl.CostEstimate(flops=OPTS['cq'], bytes_accessed=0, transcendentals=0),
        compiler_params=pltpu.CompilerParams(vmem_limit_bytes=VMEM_MOST),
    )(*([after(cand_feat, split[0])] if OPTS['qs'] else [cand_feat]), user_row, gain_in, w_uq[0])
    arrived = over_users(queries)

    returned, first, env = [], 0, {}
    env.update({'qx': arrived[1], 'qy': arrived[2], 'qd': arrived[3], 'q': queries[0]})

    def gated(value, keys):
        ready = [env[k] for k in keys]
        return after(value, *ready) if ready else value

    for chunk, wide in enumerate(wides):
        held = {0: split[chunk]}
        far = near = split[chunk]
        if chunk:
            c = str(chunk - 1)
            far = gated(far, [k + c if k in 'maf' else k for k in OPTS['m1']])
            near = gated(near, [k + c if k in 'maf' else k for k in OPTS['a1']])
        for d in [3, 1, 2] + list(range(4, chips)):
            held[d] = over_z(held[3], 1) if d == 2 else over_z(near if d == 1 else far, d)
        env.update({'a' + str(chunk): held[1], 'm' + str(chunk): held[3], 'f' + str(chunk): held[2]})
        if chunk == 0:
            gate, pick = call(
                functools.partial(gate_kernel, cap, users), "gate",
                [HBM] * 4,
                [shape(rows, width, dtype=jnp.float32), shape(rows, users * cap)],
                operands + [pltpu.SemaphoreType.DMA((3 + SLICES,))],
                OPTS['cg'],
                gated(cand_feat, ['q'] + OPTS['g']), user_row, gain_in, w_uq[0], vmem=VMEM_MOST,
            )
            env['g'] = gate
        blocks = []
        for d in range(chips):
            keys = OPTS['s0' if chunk == 0 else 's1'][d % 4]
            blocks += [held[d], over_cores(gated(held[d], keys))]
        scored = call(
            functools.partial(attend_kernel, users, chips, first), "attend",
            [SMEM] + [ANY] * (users + 2 * chips),
            [shape(cap, wide)] * users,
            [
                pltpu.VMEM((users * cap, wide), bf16),
                pltpu.VMEM((chips * BLK, 2 * wide), bf16),
                pltpu.SemaphoreType.DMA((users,)),
                pltpu.SemaphoreType.DMA((2 * chips,)),
            ],
            OPTS['ca'],
            hist_mask, *arrived, *blocks,
        )
        back = over_users(scored)
        env.update({'s': scored[0], 'rx': back[1], 'ry': back[2], 'rd': back[3]})
        returned += back
        first += wide

    return call(
        functools.partial(finish_kernel, users), "finish",
        [ANY] * (5 + len(returned)),
        [shape(rows, width)],
        [
            pltpu.VMEM((users * cap, width), bf16),
            pltpu.VMEM((rows, users * cap), bf16),
            pltpu.VMEM((rows, width), jnp.float32),
            pltpu.VMEM((1, width), jnp.float32),
            pltpu.VMEM((width, width), bf16),
            pltpu.VMEM((rows, width), bf16),
            pltpu.SemaphoreType.DMA((5 + len(returned),)),
        ],
        OPTS['cf'],
        cand_feat, gate, pick, gain_attn, w_out[0], *returned,
    )[0]


def solution(mesh):
    in_specs = (
        P(("users", "ctx"), None),
        P(("users", "ctx"), None),
        P(None, "users", "ctx", None),
        P("users", None),
        P(),
        P(),
        P(),
        P(),
    )
    out_specs = P(("users", "ctx"), None)
    return jax.shard_map(
        on_device, mesh=mesh, in_specs=in_specs, out_specs=out_specs, check_vma=False
    )
```

```python
import functools

import jax
import jax.numpy as jnp
from jax import lax
from jax.experimental import pallas as pl
from jax.experimental.pallas import tpu as pltpu
from jax.sharding import PartitionSpec as P

BLK = 128
HEAD = 128
OPTS = {'chunks': [4, 4], 'order': 0, 'qs': 1, 'cq': 0, 'cg': 400000000000, 'ca': 2000000000, 'cf': 400000000000, 'cp': 0, 'sw': [0, 0], 'p0': [], 'p1': [], 'm1': ['m', 'a'], 'a1': ['f', 'g'], 'g': [], 's0': [['qx'], [], ['g'], ['g', 'qx']], 's1': [[], ['s'], ['rd'], []]}
CHUNKS = OPTS['chunks']
SLICES = 2
VMEM_LIMIT = 32 * 1024 * 1024
VMEM_MOST = 60 * 1024 * 1024
HEAVY = 4 * 10**11


def silu_halved(t):
    return t + t * jnp.tanh(t)


def centred_norm(x):
    middle = jnp.mean(x, axis=-1, keepdims=True)
    shifted = x - middle
    spread = jnp.mean(shifted * shifted, axis=-1, keepdims=True)
    return shifted * lax.rsqrt(spread + 1e-05)


def slots_of(user, me, cap, users):
    rows = user.shape[1]
    rel = user ^ me
    places = max(8, users)
    one_hot = rel == lax.broadcasted_iota(jnp.int32, (places, rows), 0)
    one_hot = one_hot.astype(jnp.float32)
    first = lax.broadcasted_iota(jnp.int32, (rows, rows), 0)
    second = lax.broadcasted_iota(jnp.int32, (rows, rows), 1)
    earlier = (first < second).astype(jnp.bfloat16)
    rank = jnp.dot(one_hot.astype(jnp.bfloat16), earlier, preferred_element_type=jnp.float32)
    rank = jnp.sum(rank * one_hot, axis=0, keepdims=True)
    return rel.astype(jnp.float32) * cap + rank


def kv_split_kernel(kv, *outs):
    half = kv.shape[1] // 2
    first = 0
    for out in outs:
        wide = out.shape[1] // 2
        for part in range(2):
            out[:, part * wide:(part + 1) * wide] = kv[
                :, part * half + first:part * half + first + wide
            ]
        first += wide


def load_operands(first_col, feat_in, user_in, gain_in, w_in, feat, user, gain, weights, sems):
    slices, depth, width = weights.shape
    copies = [
        pltpu.make_async_copy(user_in, user, sems.at[0]),
        pltpu.make_async_copy(feat_in, feat, sems.at[1]),
        pltpu.make_async_copy(gain_in, gain, sems.at[2]),
    ]
    for k in range(slices):
        copies.append(
            pltpu.make_async_copy(
                w_in.at[pl.ds(k * depth, depth), pl.ds(first_col, width)],
                weights.at[k],
                sems.at[3 + k],
            )
        )
    for copy in copies:
        copy.start()
    return copies


def project(copies, feat, gain, weights):
    slices, depth, _ = weights.shape
    copies[1].wait()
    copies[2].wait()
    normed = (centred_norm(feat[...].astype(jnp.float32)) * gain[...]).astype(jnp.bfloat16)
    total = None
    for k in range(slices):
        copies[3 + k].wait()
        part = jnp.dot(
            normed[:, k * depth:(k + 1) * depth], weights[k], preferred_element_type=jnp.float32
        )
        total = part if total is None else total + part
    return silu_halved(total * 0.5)


def query_kernel(cap, users, feat_in, user_in, gain_in, w_in, *rest):
    outs, (feat, user, gain, weights, sent, sems, out_sems) = rest[:users], rest[users:]
    rows, width = feat.shape
    copies = load_operands(width, feat_in, user_in, gain_in, w_in, feat, user, gain, weights, sems)
    copies[0].wait()
    slot = slots_of(user[...], lax.axis_index("users"), cap, users)
    places = lax.broadcasted_iota(jnp.int32, (users * cap, rows), 0).astype(jnp.float32)
    pick = (places == slot).astype(jnp.bfloat16)
    query = project(copies, feat, gain, weights).astype(jnp.bfloat16)
    writes = []
    for d in range(users):
        at = slice(d * cap, (d + 1) * cap)
        sent[at, :] = jnp.dot(pick[at, :], query, preferred_element_type=jnp.float32).astype(
            jnp.bfloat16
        )
        writes.append(
            pltpu.make_async_copy(sent.at[pl.ds(d * cap, cap), :], outs[d], out_sems.at[d])
        )
        writes[-1].start()
    for write in writes:
        write.wait()


def gate_kernel(cap, users, feat_in, user_in, gain_in, w_in, gate, pick, feat, user, gain, weights, sems):
    rows, _ = feat.shape
    copies = load_operands(0, feat_in, user_in, gain_in, w_in, feat, user, gain, weights, sems)
    copies[0].wait()
    slot = slots_of(user[...], lax.axis_index("users"), cap, users)
    slot = jnp.transpose(jnp.broadcast_to(slot, (128, rows)))[:, 0:1]
    places = lax.broadcasted_iota(jnp.int32, (rows, users * cap), 1).astype(jnp.float32)
    pick[...] = (places == slot).astype(jnp.bfloat16)
    gate[...] = project(copies, feat, gain, weights)


def pack_kernel(chips, mask, *rest):
    blocks, out = rest[:-1], rest[-1]
    place = lax.axis_index("ctx")
    core, z = place % 2, place // 2
    taken = jnp.int32(0)
    for d, block in enumerate(blocks):
        live = mask[0, 2 * (z ^ d) + core] > 0

        def take(block=block, taken=taken):
            at = pl.multiple_of(taken * BLK, BLK)
            out[pl.ds(at, BLK), :] = block[...]

        pl.when(live)(take)
        taken = taken + live.astype(jnp.int32)


def attend_kernel(users, chips, mask, *rest):
    queries, (mine, other) = rest[:users], rest[users:users + 2]
    outs, (all_q, live_kv) = rest[users + 2:2 * users + 2], rest[2 * users + 2:]
    cap, wide = outs[0].shape
    core = lax.axis_index("ctx") % 2
    count = jnp.int32(0)
    for z in range(chips):
        count = count + (mask[0, 2 * z + core] > 0).astype(jnp.int32)
    for slot in range(chips):
        at = slice(slot * BLK, (slot + 1) * BLK)

        def from_mine(at=at):
            live_kv[at, :] = mine[at, :]

        def from_other(at=at, slot=slot):
            source = pl.multiple_of(jnp.maximum(slot - count, 0) * BLK, BLK)
            live_kv[at, :] = other[pl.ds(source, BLK), :]

        pl.when(slot < count)(from_mine)
        pl.when(slot >= count)(from_other)
    for i, q in enumerate(queries):
        all_q[i * cap:(i + 1) * cap, :] = q[...]
    scale = 0.5 * HEAD ** (-0.5)
    for head in range(wide // HEAD):
        cols = slice(head * HEAD, (head + 1) * HEAD)
        keys = live_kv[:, cols]
        values = live_kv[:, wide + head * HEAD:wide + (head + 1) * HEAD]
        scores = lax.dot_general(
            all_q[:, cols], keys, (((1,), (1,)), ((), ())), preferred_element_type=jnp.float32
        )
        weight = silu_halved(scores * scale).astype(jnp.bfloat16)
        got = jnp.dot(weight, values, preferred_element_type=jnp.float32).astype(jnp.bfloat16)
        for i, out in enumerate(outs):
            out[:, cols] = got[i * cap:(i + 1) * cap, :]


def attend_blocks_kernel(users, chips, mask, *rest):
    queries = rest[:users]
    blocks = rest[users:users + 2 * chips]
    outs, (all_q, live_kv) = rest[-2 - users:-2], rest[-2:]
    place = lax.axis_index("ctx")
    core, z = place % 2, place // 2
    cap, wide = outs[0].shape
    taken = jnp.int32(0)
    for d in range(chips):
        for swap in range(2):
            live = mask[0, 2 * (z ^ d) + (core ^ swap)] > 0

            def take(block=blocks[2 * d + swap], taken=taken):
                at = pl.multiple_of(taken * BLK, BLK)
                live_kv[pl.ds(at, BLK), :] = block[...]

            pl.when(live)(take)
            taken = jnp.minimum(taken + live.astype(jnp.int32), chips - 1)
    for i, q in enumerate(queries):
        all_q[i * cap:(i + 1) * cap, :] = q[...]
    scale = 0.5 * HEAD ** (-0.5)
    for head in range(wide // HEAD):
        cols = slice(head * HEAD, (head + 1) * HEAD)
        keys = live_kv[:, cols]
        values = live_kv[:, wide + head * HEAD:wide + (head + 1) * HEAD]
        scores = lax.dot_general(
            all_q[:, cols], keys, (((1,), (1,)), ((), ())), preferred_element_type=jnp.float32
        )
        weight = silu_halved(scores * scale).astype(jnp.bfloat16)
        got = jnp.dot(weight, values, preferred_element_type=jnp.float32).astype(jnp.bfloat16)
        for i, out in enumerate(outs):
            out[:, cols] = got[i * cap:(i + 1) * cap, :]


def finish_kernel(users, feat, gate, pick, gain, w_out, *rest):
    parts, out, back = rest[:-2], rest[-2], rest[-1]
    first = 0
    for chunk in range(len(parts) // users):
        cap, wide = parts[chunk * users].shape
        for d in range(users):
            part = parts[chunk * users + d]
            back[d * cap:(d + 1) * cap, first:first + wide] = part[...]
        first += wide
    attended = jnp.dot(pick[...], back[...], preferred_element_type=jnp.float32)
    mixed = (centred_norm(attended) * gain[...] * gate[...]).astype(jnp.bfloat16)
    grown = jnp.dot(mixed, w_out[...], preferred_element_type=jnp.float32)
    out[...] = (feat[...].astype(jnp.float32) + grown).astype(jnp.bfloat16)


SMEM = pl.BlockSpec(memory_space=pltpu.SMEM)
HBM = pl.BlockSpec(memory_space=pltpu.HBM)


def whole(*dims, at=None):
    return pl.BlockSpec(dims, lambda i: at or (0,) * len(dims))


def call(kernel, name, in_specs, out_shape, scratch, flops, *args, vmem=VMEM_LIMIT):
    moved = sum(a.size * a.dtype.itemsize for a in args)
    return pl.pallas_call(
        kernel,
        name=name,
        grid=(1,),
        in_specs=in_specs,
        out_specs=[whole(*s.shape) for s in out_shape],
        out_shape=out_shape,
        scratch_shapes=scratch,
        cost_estimate=pl.CostEstimate(flops=flops, bytes_accessed=moved if flops else 0, transcendentals=0),
        compiler_params=pltpu.CompilerParams(vmem_limit_bytes=vmem),
    )(*args)


def on_device(cand_feat, cand_user, hist_kv, hist_mask, gain_in, w_uq, gain_attn, w_out):
    users = lax.axis_size("users")
    ctx = lax.axis_size("ctx")
    chips = ctx // 2
    rows, width = cand_feat.shape
    cap = 2 * rows // users
    wides = [heads * HEAD for heads in CHUNKS]
    bf16 = jnp.bfloat16
    user_row = cand_user.reshape(1, rows)

    def shape(*dims, dtype=bf16):
        return jax.ShapeDtypeStruct(dims, dtype)

    def over_z(value, d):
        return lax.ppermute(value, "ctx", [(c, c ^ (2 * d)) for c in range(ctx)])

    def over_cores(value):
        return lax.ppermute(value, "ctx", [(c, c ^ 1) for c in range(ctx)])

    def to_user(value, d):
        return lax.ppermute(value, "users", [(u, u ^ d) for u in range(users)])

    def after(value, *others):
        return lax.optimization_barrier((value, *others))[0]

    def over_users(values):
        if OPTS['order'] == 0:
            got = [to_user(values[d], d) for d in range(users - 1, 0, -1)]
            return [values[0]] + got[::-1]
        return [values[0]] + [to_user(values[d], d) for d in range(1, users)]

    kv = hist_kv[0, 0]
    split = call(
        kv_split_kernel, "kv_split", [whole(*kv.shape)],
        [shape(BLK, 2 * wide) for wide in wides], [], 0, kv,
    )

    operands = [
        pltpu.VMEM((rows, width), bf16),
        pltpu.VMEM((1, rows), jnp.int32),
        pltpu.VMEM((1, width), jnp.float32),
        pltpu.VMEM((SLICES, width // SLICES, width), bf16),
    ]
    queries = pl.pallas_call(
        functools.partial(query_kernel, cap, users),
        name="query",
        in_specs=[HBM] * 4,
        out_specs=[HBM] * users,
        out_shape=[shape(cap, width)] * users,
        scratch_shapes=operands + [
            pltpu.VMEM((users * cap, width), bf16),
            pltpu.SemaphoreType.DMA((3 + SLICES,)),
            pltpu.SemaphoreType.DMA((users,)),
        ],
        cost_estimate=pl.CostEstimate(flops=OPTS['cq'], bytes_accessed=0, transcendentals=0),
        compiler_params=pltpu.CompilerParams(vmem_limit_bytes=VMEM_MOST),
    )(*([after(cand_feat, split[0])] if OPTS['qs'] else [cand_feat]), user_row, gain_in, w_uq[0])
    arrived = over_users(queries)

    returned, first, env = [], 0, {}
    env.update({'qx': arrived[1], 'qy': arrived[2], 'qd': arrived[3], 'q': queries[0]})

    def gated(value, keys):
        ready = [env[k] for k in keys]
        return after(value, *ready) if ready else value

    for chunk, wide in enumerate(wides):
        held = {0: split[chunk]}
        far = near = split[chunk]
        if chunk:
            c = str(chunk - 1)
            far = gated(far, [k + c if k in 'maf' else k for k in OPTS['m1']])
            near = gated(near, [k + c if k in 'maf' else k for k in OPTS['a1']])
        for d in [3, 1, 2] + list(range(4, chips)):
            held[d] = over_z(held[3], 1) if d == 2 else over_z(near if d == 1 else far, d)
        env.update({'a' + str(chunk): held[1], 'm' + str(chunk): held[3], 'f' + str(chunk): held[2]})
        if chunk == 0:
            gate, pick = call(
                functools.partial(gate_kernel, cap, users), "gate",
                [HBM] * 4,
                [shape(rows, width, dtype=jnp.float32), shape(rows, users * cap)],
                operands + [pltpu.SemaphoreType.DMA((3 + SLICES,))],
                OPTS['cg'],
                gated(cand_feat, ['q'] + OPTS['g']), user_row, gain_in, w_uq[0], vmem=VMEM_MOST,
            )
            env['g'] = gate
        if OPTS['sw'][chunk]:
            keys = OPTS['p0'] if chunk == 0 else OPTS['p1']
            packed, = call(
                functools.partial(pack_kernel, chips), "pack",
                [SMEM] + [whole(BLK, 2 * wide)] * chips,
                [shape(chips * BLK, 2 * wide)], [], OPTS['cp'],
                hist_mask, gated(held[0], keys), *[held[d] for d in range(1, chips)],
            )
            blocks, kernel = [packed, over_cores(packed)], attend_kernel
        else:
            blocks, kernel = [], attend_blocks_kernel
            for d in range(chips):
                keys = OPTS['s0' if chunk == 0 else 's1'][d % 4]
                blocks += [held[d], over_cores(gated(held[d], keys))]
        scored = call(
            functools.partial(kernel, users, chips), "attend",
            [SMEM] + [whole(cap, wide, at=(0, chunk))] * users + [whole(*block.shape) for block in blocks],
            [shape(cap, wide)] * users,
            [pltpu.VMEM((users * cap, wide), bf16), pltpu.VMEM((chips * BLK, 2 * wide), bf16)],
            OPTS['ca'],
            hist_mask, *arrived, *blocks,
        )
        back = over_users(scored)
        env.update({'s': scored[0], 'rx': back[1], 'ry': back[2], 'rd': back[3]})
        returned += back
        first += wide

    return call(
        functools.partial(finish_kernel, users), "finish",
        [
            whole(rows, width), whole(rows, width), whole(rows, users * cap), whole(1, width),
            whole(width, width),
        ]
        + [whole(*part.shape) for part in returned],
        [shape(rows, width)],
        [pltpu.VMEM((users * cap, width), bf16)],
        OPTS["cf"],
        cand_feat, gate, pick, gain_attn, w_out[0], *returned,
    )[0]


def solution(mesh):
    in_specs = (
        P(("users", "ctx"), None),
        P(("users", "ctx"), None),
        P(None, "users", "ctx", None),
        P("users", None),
        P(),
        P(),
        P(),
        P(),
    )
    out_specs = P(("users", "ctx"), None)
    return jax.shard_map(
        on_device, mesh=mesh, in_specs=in_specs, out_specs=out_specs, check_vma=False
    )
```

```python
import functools

import jax
import jax.numpy as jnp
from jax import lax
from jax.experimental import pallas as pl
from jax.experimental.pallas import tpu as pltpu
from jax.sharding import PartitionSpec as P

BLK = 128
HEAD = 128
OPTS = {'chunks': [4, 4], 'order': 0, 'qs': 1, 'cq': 0, 'cg': 400000000000, 'ca': 2000000000, 'cf': 400000000000, 'cp': 0, 'sw': [0, 0], 'p0': [], 'p1': [], 'm1': [], 'a1': [], 'g': ['a0'], 's0': [['qx'], [], ['g'], ['g', 'qx']], 's1': [[], ['s'], ['rd'], []], 'cl': 400000000000}
CHUNKS = OPTS['chunks']
SLICES = 2
VMEM_LIMIT = 32 * 1024 * 1024
VMEM_MOST = 60 * 1024 * 1024
HEAVY = 4 * 10**11


def silu_halved(t):
    return t + t * jnp.tanh(t)


def centred_norm(x):
    middle = jnp.mean(x, axis=-1, keepdims=True)
    shifted = x - middle
    spread = jnp.mean(shifted * shifted, axis=-1, keepdims=True)
    return shifted * lax.rsqrt(spread + 1e-05)


def slots_of(user, me, cap, users):
    rows = user.shape[1]
    rel = user ^ me
    places = max(8, users)
    one_hot = rel == lax.broadcasted_iota(jnp.int32, (places, rows), 0)
    one_hot = one_hot.astype(jnp.float32)
    first = lax.broadcasted_iota(jnp.int32, (rows, rows), 0)
    second = lax.broadcasted_iota(jnp.int32, (rows, rows), 1)
    earlier = (first < second).astype(jnp.bfloat16)
    rank = jnp.dot(one_hot.astype(jnp.bfloat16), earlier, preferred_element_type=jnp.float32)
    rank = jnp.sum(rank * one_hot, axis=0, keepdims=True)
    return rel.astype(jnp.float32) * cap + rank


def kv_split_kernel(kv, *outs):
    half = kv.shape[1] // 2
    first = 0
    for out in outs:
        wide = out.shape[1] // 2
        for part in range(2):
            out[:, part * wide:(part + 1) * wide] = kv[
                :, part * half + first:part * half + first + wide
            ]
        first += wide


def load_operands(first_col, feat_in, user_in, gain_in, w_in, feat, user, gain, weights, sems):
    slices, depth, width = weights.shape
    copies = [
        pltpu.make_async_copy(user_in, user, sems.at[0]),
        pltpu.make_async_copy(feat_in, feat, sems.at[1]),
        pltpu.make_async_copy(gain_in, gain, sems.at[2]),
    ]
    for k in range(slices):
        copies.append(
            pltpu.make_async_copy(
                w_in.at[pl.ds(k * depth, depth), pl.ds(first_col, width)],
                weights.at[k],
                sems.at[3 + k],
            )
        )
    for copy in copies:
        copy.start()
    return copies


def project(copies, feat, gain, weights):
    slices, depth, _ = weights.shape
    copies[1].wait()
    copies[2].wait()
    normed = (centred_norm(feat[...].astype(jnp.float32)) * gain[...]).astype(jnp.bfloat16)
    total = None
    for k in range(slices):
        copies[3 + k].wait()
        part = jnp.dot(
            normed[:, k * depth:(k + 1) * depth], weights[k], preferred_element_type=jnp.float32
        )
        total = part if total is None else total + part
    return silu_halved(total * 0.5)


def query_kernel(cap, users, feat_in, user_in, gain_in, w_in, *rest):
    outs, (feat, user, gain, weights, sent, sems, out_sems) = rest[:users], rest[users:]
    rows, width = feat.shape
    copies = load_operands(width, feat_in, user_in, gain_in, w_in, feat, user, gain, weights, sems)
    copies[0].wait()
    slot = slots_of(user[...], lax.axis_index("users"), cap, users)
    places = lax.broadcasted_iota(jnp.int32, (users * cap, rows), 0).astype(jnp.float32)
    pick = (places == slot).astype(jnp.bfloat16)
    query = project(copies, feat, gain, weights).astype(jnp.bfloat16)
    writes = []
    for d in range(users):
        at = slice(d * cap, (d + 1) * cap)
        sent[at, :] = jnp.dot(pick[at, :], query, preferred_element_type=jnp.float32).astype(
            jnp.bfloat16
        )
        writes.append(
            pltpu.make_async_copy(sent.at[pl.ds(d * cap, cap), :], outs[d], out_sems.at[d])
        )
        writes[-1].start()
    for write in writes:
        write.wait()


def gate_kernel(feat_in, user_in, gain_in, w_in, gate, feat, user, gain, weights, sems):
    copies = load_operands(0, feat_in, user_in, gain_in, w_in, feat, user, gain, weights, sems)
    copies[0].wait()
    gate[...] = project(copies, feat, gain, weights)


def pick_kernel(cap, users, user, pick):
    rows = user.shape[1]
    slot = slots_of(user[...], lax.axis_index("users"), cap, users)
    slot = jnp.transpose(jnp.broadcast_to(slot, (128, rows)))[:, 0:1]
    places = lax.broadcasted_iota(jnp.int32, (rows, users * cap), 1).astype(jnp.float32)
    pick[...] = (places == slot).astype(jnp.bfloat16)


def pack_kernel(chips, mask, *rest):
    blocks, out = rest[:-1], rest[-1]
    place = lax.axis_index("ctx")
    core, z = place % 2, place // 2
    taken = jnp.int32(0)
    for d, block in enumerate(blocks):
        live = mask[0, 2 * (z ^ d) + core] > 0

        def take(block=block, taken=taken):
            at = pl.multiple_of(taken * BLK, BLK)
            out[pl.ds(at, BLK), :] = block[...]

        pl.when(live)(take)
        taken = taken + live.astype(jnp.int32)


def attend_kernel(users, chips, mask, *rest):
    queries, (mine, other) = rest[:users], rest[users:users + 2]
    outs, (all_q, live_kv) = rest[users + 2:2 * users + 2], rest[2 * users + 2:]
    cap, wide = outs[0].shape
    core = lax.axis_index("ctx") % 2
    count = jnp.int32(0)
    for z in range(chips):
        count = count + (mask[0, 2 * z + core] > 0).astype(jnp.int32)
    for slot in range(chips):
        at = slice(slot * BLK, (slot + 1) * BLK)

        def from_mine(at=at):
            live_kv[at, :] = mine[at, :]

        def from_other(at=at, slot=slot):
            source = pl.multiple_of(jnp.maximum(slot - count, 0) * BLK, BLK)
            live_kv[at, :] = other[pl.ds(source, BLK), :]

        pl.when(slot < count)(from_mine)
        pl.when(slot >= count)(from_other)
    for i, q in enumerate(queries):
        all_q[i * cap:(i + 1) * cap, :] = q[...]
    scale = 0.5 * HEAD ** (-0.5)
    for head in range(wide // HEAD):
        cols = slice(head * HEAD, (head + 1) * HEAD)
        keys = live_kv[:, cols]
        values = live_kv[:, wide + head * HEAD:wide + (head + 1) * HEAD]
        scores = lax.dot_general(
            all_q[:, cols], keys, (((1,), (1,)), ((), ())), preferred_element_type=jnp.float32
        )
        weight = silu_halved(scores * scale).astype(jnp.bfloat16)
        got = jnp.dot(weight, values, preferred_element_type=jnp.float32).astype(jnp.bfloat16)
        for i, out in enumerate(outs):
            out[:, cols] = got[i * cap:(i + 1) * cap, :]


def attend_blocks_kernel(users, chips, mask, *rest):
    queries = rest[:users]
    blocks = rest[users:users + 2 * chips]
    outs, (all_q, live_kv) = rest[-2 - users:-2], rest[-2:]
    place = lax.axis_index("ctx")
    core, z = place % 2, place // 2
    cap, wide = outs[0].shape
    taken = jnp.int32(0)
    for d in range(chips):
        for swap in range(2):
            live = mask[0, 2 * (z ^ d) + (core ^ swap)] > 0

            def take(block=blocks[2 * d + swap], taken=taken):
                at = pl.multiple_of(taken * BLK, BLK)
                live_kv[pl.ds(at, BLK), :] = block[...]

            pl.when(live)(take)
            taken = jnp.minimum(taken + live.astype(jnp.int32), chips - 1)
    for i, q in enumerate(queries):
        all_q[i * cap:(i + 1) * cap, :] = q[...]
    scale = 0.5 * HEAD ** (-0.5)
    for head in range(wide // HEAD):
        cols = slice(head * HEAD, (head + 1) * HEAD)
        keys = live_kv[:, cols]
        values = live_kv[:, wide + head * HEAD:wide + (head + 1) * HEAD]
        scores = lax.dot_general(
            all_q[:, cols], keys, (((1,), (1,)), ((), ())), preferred_element_type=jnp.float32
        )
        weight = silu_halved(scores * scale).astype(jnp.bfloat16)
        got = jnp.dot(weight, values, preferred_element_type=jnp.float32).astype(jnp.bfloat16)
        for i, out in enumerate(outs):
            out[:, cols] = got[i * cap:(i + 1) * cap, :]


def finish_kernel(users, feat, gate, pick, gain, w_out, *rest):
    parts, out, back = rest[:-2], rest[-2], rest[-1]
    first = 0
    for chunk in range(len(parts) // users):
        cap, wide = parts[chunk * users].shape
        for d in range(users):
            part = parts[chunk * users + d]
            back[d * cap:(d + 1) * cap, first:first + wide] = part[...]
        first += wide
    attended = jnp.dot(pick[...], back[...], preferred_element_type=jnp.float32)
    mixed = (centred_norm(attended) * gain[...] * gate[...]).astype(jnp.bfloat16)
    grown = jnp.dot(mixed, w_out[...], preferred_element_type=jnp.float32)
    out[...] = (feat[...].astype(jnp.float32) + grown).astype(jnp.bfloat16)


SMEM = pl.BlockSpec(memory_space=pltpu.SMEM)
HBM = pl.BlockSpec(memory_space=pltpu.HBM)


def whole(*dims, at=None):
    return pl.BlockSpec(dims, lambda i: at or (0,) * len(dims))


def call(kernel, name, in_specs, out_shape, scratch, flops, *args, vmem=VMEM_LIMIT):
    moved = sum(a.size * a.dtype.itemsize for a in args)
    return pl.pallas_call(
        kernel,
        name=name,
        grid=(1,),
        in_specs=in_specs,
        out_specs=[whole(*s.shape) for s in out_shape],
        out_shape=out_shape,
        scratch_shapes=scratch,
        cost_estimate=pl.CostEstimate(flops=flops, bytes_accessed=moved if flops else 0, transcendentals=0),
        compiler_params=pltpu.CompilerParams(vmem_limit_bytes=vmem),
    )(*args)


def on_device(cand_feat, cand_user, hist_kv, hist_mask, gain_in, w_uq, gain_attn, w_out):
    users = lax.axis_size("users")
    ctx = lax.axis_size("ctx")
    chips = ctx // 2
    rows, width = cand_feat.shape
    cap = 2 * rows // users
    wides = [heads * HEAD for heads in CHUNKS]
    bf16 = jnp.bfloat16
    user_row = cand_user.reshape(1, rows)

    def shape(*dims, dtype=bf16):
        return jax.ShapeDtypeStruct(dims, dtype)

    def over_z(value, d):
        return lax.ppermute(value, "ctx", [(c, c ^ (2 * d)) for c in range(ctx)])

    def over_cores(value):
        return lax.ppermute(value, "ctx", [(c, c ^ 1) for c in range(ctx)])

    def to_user(value, d):
        return lax.ppermute(value, "users", [(u, u ^ d) for u in range(users)])

    def after(value, *others):
        return lax.optimization_barrier((value, *others))[0]

    def over_users(values):
        if OPTS['order'] == 0:
            got = [to_user(values[d], d) for d in range(users - 1, 0, -1)]
            return [values[0]] + got[::-1]
        return [values[0]] + [to_user(values[d], d) for d in range(1, users)]

    kv = hist_kv[0, 0]
    split = call(
        kv_split_kernel, "kv_split", [whole(*kv.shape)],
        [shape(BLK, 2 * wide) for wide in wides], [], 0, kv,
    )

    operands = [
        pltpu.VMEM((rows, width), bf16),
        pltpu.VMEM((1, rows), jnp.int32),
        pltpu.VMEM((1, width), jnp.float32),
        pltpu.VMEM((SLICES, width // SLICES, width), bf16),
    ]
    queries = pl.pallas_call(
        functools.partial(query_kernel, cap, users),
        name="query",
        in_specs=[HBM] * 4,
        out_specs=[HBM] * users,
        out_shape=[shape(cap, width)] * users,
        scratch_shapes=operands + [
            pltpu.VMEM((users * cap, width), bf16),
            pltpu.SemaphoreType.DMA((3 + SLICES,)),
            pltpu.SemaphoreType.DMA((users,)),
        ],
        cost_estimate=pl.CostEstimate(flops=OPTS['cq'], bytes_accessed=0, transcendentals=0),
        compiler_params=pltpu.CompilerParams(vmem_limit_bytes=VMEM_MOST),
    )(*([after(cand_feat, split[0])] if OPTS['qs'] else [cand_feat]), user_row, gain_in, w_uq[0])
    arrived = over_users(queries)

    returned, first, env = [], 0, {}
    env.update({'qx': arrived[1], 'qy': arrived[2], 'qd': arrived[3], 'q': queries[0]})

    def gated(value, keys):
        ready = [env[k] for k in keys]
        return after(value, *ready) if ready else value

    for chunk, wide in enumerate(wides):
        held = {0: split[chunk]}
        far = near = split[chunk]
        if chunk:
            c = str(chunk - 1)
            far = gated(far, [k + c if k in 'maf' else k for k in OPTS['m1']])
            near = gated(near, [k + c if k in 'maf' else k for k in OPTS['a1']])
        for d in [3, 1, 2] + list(range(4, chips)):
            held[d] = over_z(held[3], 1) if d == 2 else over_z(near if d == 1 else far, d)
        env.update({'a' + str(chunk): held[1], 'm' + str(chunk): held[3], 'f' + str(chunk): held[2]})
        if chunk == 0:
            pick, = call(
                functools.partial(pick_kernel, cap, users), "pick", [whole(1, rows)],
                [shape(rows, users * cap)], [], OPTS['cg'],
                gated(user_row, ['q'] + OPTS['g']), vmem=VMEM_MOST,
            )
            env['g'] = pick
        if OPTS['sw'][chunk]:
            keys = OPTS['p0'] if chunk == 0 else OPTS['p1']
            packed, = call(
                functools.partial(pack_kernel, chips), "pack",
                [SMEM] + [whole(BLK, 2 * wide)] * chips,
                [shape(chips * BLK, 2 * wide)], [], OPTS['cp'],
                hist_mask, gated(held[0], keys), *[held[d] for d in range(1, chips)],
            )
            blocks, kernel = [packed, over_cores(packed)], attend_kernel
        else:
            blocks, kernel = [], attend_blocks_kernel
            for d in range(chips):
                keys = OPTS['s0' if chunk == 0 else 's1'][d % 4]
                blocks += [held[d], over_cores(gated(held[d], keys))]
        scored = call(
            functools.partial(kernel, users, chips), "attend",
            [SMEM] + [whole(cap, wide, at=(0, chunk))] * users + [whole(*block.shape) for block in blocks],
            [shape(cap, wide)] * users,
            [pltpu.VMEM((users * cap, wide), bf16), pltpu.VMEM((chips * BLK, 2 * wide), bf16)],
            OPTS['ca'],
            hist_mask, *arrived, *blocks,
        )
        back = over_users(scored)
        env.update({'s': scored[0], 'rx': back[1], 'ry': back[2], 'rd': back[3]})
        returned += back
        first += wide

    gate, = call(
        gate_kernel, "gate", [HBM] * 4, [shape(rows, width, dtype=jnp.float32)],
        operands + [pltpu.SemaphoreType.DMA((3 + SLICES,))],
        OPTS['cl'],
        after(cand_feat, scored[0]), user_row, gain_in, w_uq[0], vmem=VMEM_MOST,
    )
    return call(
        functools.partial(finish_kernel, users), "finish",
        [
            whole(rows, width), whole(rows, width), whole(rows, users * cap), whole(1, width),
            whole(width, width),
        ]
        + [whole(*part.shape) for part in returned],
        [shape(rows, width)],
        [pltpu.VMEM((users * cap, width), bf16)],
        OPTS["cf"],
        cand_feat, gate, pick, gain_attn, w_out[0], *returned,
    )[0]


def solution(mesh):
    in_specs = (
        P(("users", "ctx"), None),
        P(("users", "ctx"), None),
        P(None, "users", "ctx", None),
        P("users", None),
        P(),
        P(),
        P(),
        P(),
    )
    out_specs = P(("users", "ctx"), None)
    return jax.shard_map(
        on_device, mesh=mesh, in_specs=in_specs, out_specs=out_specs, check_vma=False
    )
```

```python
import functools

import jax
import jax.numpy as jnp
from jax import lax
from jax.experimental import pallas as pl
from jax.experimental.pallas import tpu as pltpu
from jax.sharding import PartitionSpec as P

BLK = 128
HEAD = 128
CHUNKS = (4, 4)
SLICES = 2
VMEM_LIMIT = 32 * 1024 * 1024
VMEM_MOST = 60 * 1024 * 1024
HEAVY = 4 * 10**11


def silu_halved(t):
    return t + t * jnp.tanh(t)


def centred_norm(x):
    middle = jnp.mean(x, axis=-1, keepdims=True)
    shifted = x - middle
    spread = jnp.mean(shifted * shifted, axis=-1, keepdims=True)
    return shifted * lax.rsqrt(spread + 1e-05)


def slots_of(user, me, cap, users):
    rows = user.shape[1]
    rel = user ^ me
    places = max(8, users)
    one_hot = rel == lax.broadcasted_iota(jnp.int32, (places, rows), 0)
    one_hot = one_hot.astype(jnp.float32)
    first = lax.broadcasted_iota(jnp.int32, (rows, rows), 0)
    second = lax.broadcasted_iota(jnp.int32, (rows, rows), 1)
    earlier = (first < second).astype(jnp.bfloat16)
    rank = jnp.dot(one_hot.astype(jnp.bfloat16), earlier, preferred_element_type=jnp.float32)
    rank = jnp.sum(rank * one_hot, axis=0, keepdims=True)
    return rel.astype(jnp.float32) * cap + rank


def kv_split_kernel(kv, *outs):
    half = kv.shape[1] // 2
    first = 0
    for out in outs:
        wide = out.shape[1] // 2
        for part in range(2):
            out[:, part * wide:(part + 1) * wide] = kv[
                :, part * half + first:part * half + first + wide
            ]
        first += wide


def load_operands(first_col, feat_in, user_in, gain_in, w_in, feat, user, gain, weights, sems):
    slices, depth, width = weights.shape
    copies = [
        pltpu.make_async_copy(user_in, user, sems.at[0]),
        pltpu.make_async_copy(feat_in, feat, sems.at[1]),
        pltpu.make_async_copy(gain_in, gain, sems.at[2]),
    ]
    for k in range(slices):
        copies.append(
            pltpu.make_async_copy(
                w_in.at[pl.ds(k * depth, depth), pl.ds(first_col, width)],
                weights.at[k],
                sems.at[3 + k],
            )
        )
    for copy in copies:
        copy.start()
    return copies


def project(copies, feat, gain, weights):
    slices, depth, _ = weights.shape
    copies[1].wait()
    copies[2].wait()
    normed = (centred_norm(feat[...].astype(jnp.float32)) * gain[...]).astype(jnp.bfloat16)
    total = None
    for k in range(slices):
        copies[3 + k].wait()
        part = jnp.dot(
            normed[:, k * depth:(k + 1) * depth], weights[k], preferred_element_type=jnp.float32
        )
        total = part if total is None else total + part
    return silu_halved(total * 0.5)


def query_kernel(cap, users, feat_in, user_in, gain_in, w_in, *rest):
    outs, (feat, user, gain, weights, sent, sems, out_sems) = rest[:users], rest[users:]
    rows, width = feat.shape
    copies = load_operands(width, feat_in, user_in, gain_in, w_in, feat, user, gain, weights, sems)
    copies[0].wait()
    slot = slots_of(user[...], lax.axis_index("users"), cap, users)
    places = lax.broadcasted_iota(jnp.int32, (users * cap, rows), 0).astype(jnp.float32)
    pick = (places == slot).astype(jnp.bfloat16)
    query = project(copies, feat, gain, weights).astype(jnp.bfloat16)
    writes = []
    for d in range(users):
        at = slice(d * cap, (d + 1) * cap)
        sent[at, :] = jnp.dot(pick[at, :], query, preferred_element_type=jnp.float32).astype(
            jnp.bfloat16
        )
        writes.append(
            pltpu.make_async_copy(sent.at[pl.ds(d * cap, cap), :], outs[d], out_sems.at[d])
        )
        writes[-1].start()
    for write in writes:
        write.wait()


def gate_kernel(cap, users, feat_in, user_in, gain_in, w_in, gate, pick, feat, user, gain, weights, sems):
    rows, _ = feat.shape
    copies = load_operands(0, feat_in, user_in, gain_in, w_in, feat, user, gain, weights, sems)
    copies[0].wait()
    slot = slots_of(user[...], lax.axis_index("users"), cap, users)
    slot = jnp.transpose(jnp.broadcast_to(slot, (128, rows)))[:, 0:1]
    places = lax.broadcasted_iota(jnp.int32, (rows, users * cap), 1).astype(jnp.float32)
    pick[...] = (places == slot).astype(jnp.bfloat16)
    gate[...] = project(copies, feat, gain, weights)


def attend_kernel(users, chips, mask, *rest):
    queries = rest[:users]
    blocks = rest[users:users + 2 * chips]
    outs, (all_q, live_kv) = rest[-2 - users:-2], rest[-2:]
    place = lax.axis_index("ctx")
    core, z = place % 2, place // 2
    cap, wide = outs[0].shape
    taken = jnp.int32(0)
    for d in range(chips):
        for swap in range(2):
            live = mask[0, 2 * (z ^ d) + (core ^ swap)] > 0

            def take(block=blocks[2 * d + swap], taken=taken):
                at = pl.multiple_of(taken * BLK, BLK)
                live_kv[pl.ds(at, BLK), :] = block[...]

            pl.when(live)(take)
            taken = jnp.minimum(taken + live.astype(jnp.int32), chips - 1)
    for i, q in enumerate(queries):
        all_q[i * cap:(i + 1) * cap, :] = q[...]
    scale = 0.5 * HEAD ** (-0.5)
    for head in range(wide // HEAD):
        cols = slice(head * HEAD, (head + 1) * HEAD)
        keys = live_kv[:, cols]
        values = live_kv[:, wide + head * HEAD:wide + (head + 1) * HEAD]
        scores = lax.dot_general(
            all_q[:, cols], keys, (((1,), (1,)), ((), ())), preferred_element_type=jnp.float32
        )
        weight = silu_halved(scores * scale).astype(jnp.bfloat16)
        got = jnp.dot(weight, values, preferred_element_type=jnp.float32).astype(jnp.bfloat16)
        for i, out in enumerate(outs):
            out[:, cols] = got[i * cap:(i + 1) * cap, :]


def finish_kernel(users, feat, gate, pick, gain, w_out, *rest):
    parts, out, back = rest[:-2], rest[-2], rest[-1]
    first = 0
    for chunk in range(len(parts) // users):
        cap, wide = parts[chunk * users].shape
        for d in range(users):
            part = parts[chunk * users + d]
            back[d * cap:(d + 1) * cap, first:first + wide] = part[...]
        first += wide
    attended = jnp.dot(pick[...], back[...], preferred_element_type=jnp.float32)
    mixed = (centred_norm(attended) * gain[...] * gate[...]).astype(jnp.bfloat16)
    grown = jnp.dot(mixed, w_out[...], preferred_element_type=jnp.float32)
    out[...] = (feat[...].astype(jnp.float32) + grown).astype(jnp.bfloat16)


SMEM = pl.BlockSpec(memory_space=pltpu.SMEM)
HBM = pl.BlockSpec(memory_space=pltpu.HBM)


def whole(*dims, at=None):
    return pl.BlockSpec(dims, lambda i: at or (0,) * len(dims))


def call(kernel, name, in_specs, out_shape, scratch, flops, *args, vmem=VMEM_LIMIT):
    moved = sum(a.size * a.dtype.itemsize for a in args)
    return pl.pallas_call(
        kernel,
        name=name,
        grid=(1,),
        in_specs=in_specs,
        out_specs=[whole(*s.shape) for s in out_shape],
        out_shape=out_shape,
        scratch_shapes=scratch,
        cost_estimate=pl.CostEstimate(flops=flops, bytes_accessed=moved if flops else 0, transcendentals=0),
        compiler_params=pltpu.CompilerParams(vmem_limit_bytes=vmem),
    )(*args)


def on_device(cand_feat, cand_user, hist_kv, hist_mask, gain_in, w_uq, gain_attn, w_out):
    users = lax.axis_size("users")
    ctx = lax.axis_size("ctx")
    chips = ctx // 2
    rows, width = cand_feat.shape
    cap = 2 * rows // users
    wides = [heads * HEAD for heads in CHUNKS]
    bf16 = jnp.bfloat16
    user_row = cand_user.reshape(1, rows)

    def shape(*dims, dtype=bf16):
        return jax.ShapeDtypeStruct(dims, dtype)

    def over_z(value, d):
        return lax.ppermute(value, "ctx", [(c, c ^ (2 * d)) for c in range(ctx)])

    def over_cores(value):
        return lax.ppermute(value, "ctx", [(c, c ^ 1) for c in range(ctx)])

    def to_user(value, d):
        return lax.ppermute(value, "users", [(u, u ^ d) for u in range(users)])

    def after(value, *others):
        return lax.optimization_barrier((value, *others))[0]

    def over_users(values):
        got = [to_user(values[d], d) for d in range(users - 1, 0, -1)]
        return [values[0]] + got[::-1]

    kv = hist_kv[0, 0]
    split = call(
        kv_split_kernel, "kv_split", [whole(*kv.shape)],
        [shape(BLK, 2 * wide) for wide in wides], [], 0, kv,
    )

    operands = [
        pltpu.VMEM((rows, width), bf16),
        pltpu.VMEM((1, rows), jnp.int32),
        pltpu.VMEM((1, width), jnp.float32),
        pltpu.VMEM((SLICES, width // SLICES, width), bf16),
    ]
    queries = pl.pallas_call(
        functools.partial(query_kernel, cap, users),
        name="query",
        in_specs=[HBM] * 4,
        out_specs=[HBM] * users,
        out_shape=[shape(cap, width)] * users,
        scratch_shapes=operands + [
            pltpu.VMEM((users * cap, width), bf16),
            pltpu.SemaphoreType.DMA((3 + SLICES,)),
            pltpu.SemaphoreType.DMA((users,)),
        ],
        cost_estimate=pl.CostEstimate(flops=0, bytes_accessed=0, transcendentals=0),
        compiler_params=pltpu.CompilerParams(vmem_limit_bytes=VMEM_MOST),
    )(after(cand_feat, split[0]), user_row, gain_in, w_uq[0])
    arrived = over_users(queries)

    returned, first = [], None
    for chunk, wide in enumerate(wides):
        held = {0: split[chunk]}
        far = near = split[chunk]
        if chunk:
            far = after(far, first[3], first[1])
            near = after(near, first[2], gate)
        for d in [3, 1, 2] + list(range(4, chips)):
            held[d] = over_z(held[3], 1) if d == 2 else over_z(near if d == 1 else far, d)
        if chunk == 0:
            first = held
            gate, pick = call(
                functools.partial(gate_kernel, cap, users), "gate",
                [HBM] * 4,
                [shape(rows, width, dtype=jnp.float32), shape(rows, users * cap)],
                operands + [pltpu.SemaphoreType.DMA((3 + SLICES,))],
                HEAVY,
                after(cand_feat, queries[0]), user_row, gain_in, w_uq[0], vmem=VMEM_MOST,
            )
            waits = {0: [arrived[1]], 2: [gate], 3: [gate, arrived[1]]}
        else:
            waits = {1: [scored[0]], 2: [returned[3]]}
        blocks = []
        for d in range(chips):
            own = after(held[d], *waits[d]) if d in waits else held[d]
            blocks += [held[d], over_cores(own)]
        scored = call(
            functools.partial(attend_kernel, users, chips), "attend",
            [SMEM]
            + [whole(cap, wide, at=(0, chunk))] * users
            + [whole(*block.shape) for block in blocks],
            [shape(cap, wide)] * users,
            [pltpu.VMEM((users * cap, wide), bf16), pltpu.VMEM((chips * BLK, 2 * wide), bf16)],
            2 * 10**9,
            hist_mask, *arrived, *blocks,
        )
        returned += over_users(scored)

    return call(
        functools.partial(finish_kernel, users), "finish",
        [
            whole(rows, width), whole(rows, width), whole(rows, users * cap), whole(1, width),
            whole(width, width),
        ]
        + [whole(*part.shape) for part in returned],
        [shape(rows, width)],
        [pltpu.VMEM((users * cap, width), bf16)],
        HEAVY,
        cand_feat, gate, pick, gain_attn, w_out[0], *returned,
    )[0]


def solution(mesh):
    in_specs = (
        P(("users", "ctx"), None),
        P(("users", "ctx"), None),
        P(None, "users", "ctx", None),
        P("users", None),
        P(),
        P(),
        P(),
        P(),
    )
    out_specs = P(("users", "ctx"), None)
    return jax.shard_map(
        on_device, mesh=mesh, in_specs=in_specs, out_specs=out_specs, check_vma=False
    )
```
